512 devices in a mesh: rows: 512 (over z, y, x, core).
Axes of the slice: x: 4, y: 8, z: 8, core: 2. Of those that a mesh axis runs over, the one named last changes fastest.
Arguments:
- slab: bfloat16 [131072, 4096], P('rows'), may hold values from -100 to 100
- sketch_matrix: bfloat16 [64, 4096], replicated, may hold values from -0.09375 to 0.09375
Outputs:
- q_basis: bfloat16 [64, 131072], P(None, 'rows')
- projection: float32 [64, 4096], replicated
- triangle: float32 [64, 64], replicated
- gram: float32 [64, 64], replicated
The draws below stay inside these ranges and needn't reach their ends.
All inputs are finite; a program needn't handle non-finite values.
Results may differ from the reference program's by a relative error of at most 0.002.
Values sent between devices are 32-bit elements; how exact they have to be, the bound alone decides.
No kernel may reach another device: no remote copies, remote signals or barrier semaphores. Data moves between devices by JAX's collectives and lax.ppermute only.
A program may use at most 64 MiB of HBM per device.

```python
import math
import jax
import jax.numpy as jnp
from jax import lax

N = 4096
RANK = 64
TOTAL_ROWS = 131072


def draw_slab(key, part):
    key = jax.random.fold_in(key, 11)
    key_base, key_rows, key_cols = jax.random.split(key, 3)
    position = jnp.arange(TOTAL_ROWS, dtype=jnp.float32) / TOTAL_ROWS
    trend = jnp.sqrt(1.0 + 2.0 * position)[:, None]
    base = jax.random.normal(key_base, (TOTAL_ROWS, N), jnp.float32)
    row_scale = jnp.exp(jax.random.uniform(key_rows, (TOTAL_ROWS, 1), jnp.float32, math.log(0.3), math.log(3.0)))
    col_scale = jnp.exp(jax.random.uniform(key_cols, (1, N), jnp.float32, math.log(0.3), math.log(3.0)))
    return (base * row_scale * trend * col_scale).astype(jnp.bfloat16)


def normal_values(rng, dims, scale, most, kind=jnp.bfloat16):
    return jnp.clip(scale * jax.random.normal(rng, dims, jnp.float32), -most, most).astype(kind)


def setup_inputs(seed: int = 0) -> dict:
    key_of = jax.random.split(jax.random.key(seed), 3)
    slab = draw_slab(jax.random.fold_in(key_of[2], 71), 0)
    sketch_matrix = normal_values(key_of[1], (RANK, N), N ** -0.5, 0.09375)
    return dict(slab=slab, sketch_matrix=sketch_matrix)


def reference(slab, sketch_matrix):
    total = slab.shape[0]
    sketch_t = lax.dot_general(sketch_matrix.astype(jnp.float32), slab.astype(jnp.float32), (((1,), (1,)), ((), ())), preferred_element_type=jnp.float32)
    sketch_low = sketch_t.astype(jnp.bfloat16)
    cross = jnp.dot(sketch_low.astype(jnp.float32), slab.astype(jnp.float32), preferred_element_type=jnp.float32)
    folded = jnp.dot(cross.astype(jnp.float32), sketch_matrix.astype(jnp.float32).T.astype(jnp.float32), precision=lax.Precision.HIGHEST, preferred_element_type=jnp.float32)
    row_gram = 0.5 * (folded + folded.T)
    lower = jnp.linalg.cholesky(row_gram) / math.sqrt(total)
    basis_t = lax.linalg.triangular_solve(lower, sketch_t, left_side=True, lower=True)
    q_basis = basis_t.astype(jnp.bfloat16)
    projection = lax.linalg.triangular_solve(lower, cross, left_side=True, lower=True) / math.sqrt(total)
    gram = jnp.dot(projection.astype(jnp.float32), projection.T.astype(jnp.float32), precision=lax.Precision.HIGHEST, preferred_element_type=jnp.float32) / slab.shape[1]
    return (q_basis, projection, lower.T, gram)
```

```python
import math

import jax
import jax.numpy as jnp
from jax import lax
from jax.sharding import PartitionSpec as P

SIZES = dict(z=8, y=8, x=4, c=2)


def groups(axes):
    out = {}
    for index in range(math.prod(SIZES.values())):
        rest, coords = index, {}
        for name in reversed(SIZES):
            rest, coords[name] = divmod(rest, SIZES[name])
        key = tuple(value for name, value in coords.items() if name not in axes)
        out.setdefault(key, []).append(index)
    return list(out.values())


def exchange(pieces, axes):
    return lax.all_to_all(pieces, "rows", 0, 0, axis_index_groups=groups(axes), tiled=True)


def scatter_sum(tiles, axes):
    count = math.prod(SIZES[a] for a in axes)
    got = exchange(tiles, axes)
    return got.reshape(count, tiles.shape[0] // count, 8, 128).sum(0)


def spread(tiles, axes):
    count = math.prod(SIZES[a] for a in axes)
    return exchange(jnp.tile(tiles, (count, 1, 1)), axes)


def all_reduce(tiles):
    part = scatter_sum(tiles, "c")
    part = scatter_sum(part, "yx")
    size = part.shape[0]
    part = spread(part, "z").reshape(-1, size, 8, 128).sum(0)
    return spread(spread(part, "yx"), "c")


def symmetric_fold(cross_part, sketch_cols):
    folded = jnp.dot(
        cross_part,
        sketch_cols.astype(jnp.float32).T,
        precision=lax.Precision.HIGHEST,
        preferred_element_type=jnp.float32,
    )
    return 0.5 * (folded + folded.T)


def shards(slab, sketch_matrix):
    devices = lax.axis_size("rows")
    total = slab.shape[0] * devices
    columns = slab.shape[1]
    rank = sketch_matrix.shape[0]
    root = math.sqrt(total)
    sketch_t = lax.dot_general(
        sketch_matrix, slab, (((1,), (1,)), ((), ())), preferred_element_type=jnp.float32
    )
    sketch_low = sketch_t.astype(jnp.bfloat16)
    cross_part = jnp.dot(sketch_low, slab, preferred_element_type=jnp.float32)
    blocks = columns // 128
    tiles = cross_part.reshape(rank, blocks, 128).transpose(1, 0, 2).reshape(-1, 8, 128)
    tiles = all_reduce(tiles)
    cross = tiles.reshape(blocks, rank, 128).transpose(1, 0, 2).reshape(rank, columns)
    full_gram = symmetric_fold(cross, sketch_matrix)
    full_lower = jnp.linalg.cholesky(full_gram)
    lower = full_lower / root
    basis_t = lax.linalg.triangular_solve(lower, sketch_t, left_side=True, lower=True)
    q_basis = basis_t.astype(jnp.bfloat16)
    projection = lax.linalg.triangular_solve(lower, cross, left_side=True, lower=True) / root
    gram = (
        jnp.dot(
            projection,
            projection.T,
            precision=lax.Precision.HIGHEST,
            preferred_element_type=jnp.float32,
        )
        / columns
    )
    return (q_basis, projection, lower.T, gram)


def solution(mesh):
    return jax.shard_map(
        shards,
        mesh=mesh,
        in_specs=(P("rows", None), P()),
        out_specs=(P(None, "rows"), P(), P(), P()),
        check_vma=False,
    )
```

```python
import math

import jax
import jax.numpy as jnp
from jax import lax
from jax.sharding import PartitionSpec as P

SIZES = dict(z=8, y=8, x=4, c=2)


def place(index):
    coords = {}
    for name in reversed(SIZES):
        index, coords[name] = divmod(index, SIZES[name])
    return coords


def groups(axes_of_core):
    out = {}
    for index in range(math.prod(SIZES.values())):
        coords = place(index)
        axes = axes_of_core[coords["c"]]
        key = (coords["c"],) + tuple(value for name, value in coords.items() if name not in axes)
        out.setdefault(key, []).append(index)
    return list(out.values())


PLANE = groups(("yx", "zx"))
LINE = groups(("z", "y"))
PAIRS = [(i, i ^ 1) for i in range(math.prod(SIZES.values()))]


def exchange(pieces, peers):
    return lax.all_to_all(pieces, "rows", 0, 0, axis_index_groups=peers, tiled=True)


def summed(tiles, count):
    return tiles.reshape(count, tiles.shape[0] // count, 8, 128).sum(0)


def spread(tiles, peers):
    return exchange(jnp.tile(tiles, (len(peers[0]), 1, 1)), peers)


def all_reduce(tiles):
    core = lax.axis_index("rows") % 2
    half = tiles.shape[0] // 2
    give = lax.dynamic_slice_in_dim(tiles, (1 - core) * half, half)
    keep = lax.dynamic_slice_in_dim(tiles, core * half, half)
    part = keep + lax.ppermute(give, "rows", PAIRS)
    part = summed(exchange(part, PLANE), len(PLANE[0]))
    part = summed(spread(part, LINE), len(LINE[0]))
    mine = spread(part, PLANE)
    other = lax.ppermute(mine, "rows", PAIRS)
    first = core == 0
    return jnp.concatenate([jnp.where(first, mine, other), jnp.where(first, other, mine)], 0)


def symmetric_fold(cross_part, sketch_cols):
    folded = jnp.dot(
        cross_part,
        sketch_cols.astype(jnp.float32).T,
        precision=lax.Precision.HIGHEST,
        preferred_element_type=jnp.float32,
    )
    return 0.5 * (folded + folded.T)


def shards(slab, sketch_matrix):
    devices = lax.axis_size("rows")
    total = slab.shape[0] * devices
    columns = slab.shape[1]
    rank = sketch_matrix.shape[0]
    root = math.sqrt(total)
    sketch_t = lax.dot_general(
        sketch_matrix, slab, (((1,), (1,)), ((), ())), preferred_element_type=jnp.float32
    )
    sketch_low = sketch_t.astype(jnp.bfloat16)
    cross_part = jnp.dot(sketch_low, slab, preferred_element_type=jnp.float32)
    blocks = columns // 128
    tiles = cross_part.reshape(rank, blocks, 128).transpose(1, 0, 2).reshape(-1, 8, 128)
    tiles = all_reduce(tiles)
    cross = tiles.reshape(blocks, rank, 128).transpose(1, 0, 2).reshape(rank, columns)
    full_gram = symmetric_fold(cross, sketch_matrix)
    full_lower = jnp.linalg.cholesky(full_gram)
    lower = full_lower / root
    basis_t = lax.linalg.triangular_solve(lower, sketch_t, left_side=True, lower=True)
    q_basis = basis_t.astype(jnp.bfloat16)
    projection = lax.linalg.triangular_solve(lower, cross, left_side=True, lower=True) / root
    gram = (
        jnp.dot(
            projection,
            projection.T,
            precision=lax.Precision.HIGHEST,
            preferred_element_type=jnp.float32,
        )
        / columns
    )
    return (q_basis, projection, lower.T, gram)


def solution(mesh):
    return jax.shard_map(
        shards,
        mesh=mesh,
        in_specs=(P("rows", None), P()),
        out_specs=(P(None, "rows"), P(), P(), P()),
        check_vma=False,
    )
```

```python
import functools
import math

import jax
import jax.numpy as jnp
from jax import lax
from jax.experimental import pallas as pl
from jax.experimental.pallas import tpu as pltpu
from jax.sharding import PartitionSpec as P

SIZES = dict(z=8, y=8, x=4, c=2)


def place(index):
    coords = {}
    for name in reversed(SIZES):
        index, coords[name] = divmod(index, SIZES[name])
    return coords


def groups(axes_of_core):
    out = {}
    for index in range(math.prod(SIZES.values())):
        coords = place(index)
        axes = axes_of_core[coords["c"]]
        key = (coords["c"],) + tuple(value for name, value in coords.items() if name not in axes)
        out.setdefault(key, []).append(index)
    return list(out.values())


PLANE = groups(("yx", "zx"))
LINE = groups(("z", "y"))
PAIRS = [(i, i ^ 1) for i in range(math.prod(SIZES.values()))]


def exchange(pieces, peers):
    return lax.all_to_all(pieces, "rows", 0, 0, axis_index_groups=peers, tiled=True)


def summed(tiles, count):
    return tiles.reshape(count, tiles.shape[0] // count, 8, 128).sum(0)


def spread(tiles, peers):
    return exchange(jnp.tile(tiles, (len(peers[0]), 1, 1)), peers)


def all_reduce(tiles, core):
    half = tiles.shape[0] // 2
    give = lax.dynamic_slice_in_dim(tiles, (1 - core) * half, half)
    keep = lax.dynamic_slice_in_dim(tiles, core * half, half)
    part = keep + lax.ppermute(give, "rows", PAIRS)
    part = summed(exchange(part, PLANE), len(PLANE[0]))
    part = summed(spread(part, LINE), len(LINE[0]))
    mine = spread(part, PLANE)
    return mine, lax.ppermute(mine, "rows", PAIRS)


LAST = (((1,), (1,)), ((), ()))


def split(value, parts):
    out = []
    for _ in range(parts):
        out.append(value.astype(jnp.bfloat16))
        value = value - out[-1].astype(jnp.float32)
    return out


def eliminate(work, size):
    sub = lax.broadcasted_iota(jnp.int32, (8, 128), 0)

    def row(tile, k):
        return jnp.broadcast_to(tile[k : k + 1, :], (8, 128))

    work = [work[8 * b : 8 * b + 8] for b in range(work.shape[0] // 8)]
    for first in range(0, 8 * len(work), size):
        top, at = divmod(first, 8)
        live = range(top, len(work))
        column = [
            {b: jnp.broadcast_to(work[b][:, first + k : first + k + 1], (8, 128)) for b in live}
            for k in range(size)
        ]
        pivot = [row(work[top], at + k) for k in range(size)]
        m = {(i, k): row(column[k][top], at + i) for k in range(size) for i in range(k, size)}
        x, done, scaled = {}, {}, {}
        for k in range(0, size, 2):
            a, b, d = m[k, k], m[k + 1, k], m[k + 1, k + 1]
            inverse = 1.0 / (a * d - b * b)
            ai, bi, di = a * inverse, b * inverse, d * inverse
            rest = range(k + 2, size)
            for i in rest:
                x[i, k] = di * m[i, k] - bi * m[i, k + 1]
                x[i, k + 1] = ai * m[i, k + 1] - bi * m[i, k]
            for i in rest:
                for j in range(k + 2, i + 1):
                    m[i, j] = m[i, j] - x[i, k] * m[j, k] - x[i, k + 1] * m[j, k + 1]
            done[k] = pivot[k]
            done[k + 1] = pivot[k + 1] - (b * (1.0 / a)) * pivot[k]
            scaled[k] = di * pivot[k] - bi * pivot[k + 1]
            scaled[k + 1] = ai * pivot[k + 1] - bi * pivot[k]
            for i in rest:
                pivot[i] = pivot[i] - x[i, k] * pivot[k] - x[i, k + 1] * pivot[k + 1]
        for k in reversed(range(size)):
            for i in range(k // 2 * 2 + 2, size):
                scaled[k] = scaled[k] - x[i, k] * scaled[i]
        for b in live:
            new = work[b]
            if b > top or at + size < 8:
                terms = [column[k][b] * scaled[k] for k in range(size)]
                while len(terms) > 1:
                    terms = [terms[i] + terms[i + 1] for i in range(0, len(terms), 2)]
                new = new - terms[0]
            if b == top:
                new = jnp.where(sub >= at + size, new, work[b])
                for k in range(1, size):
                    new = jnp.where(sub == at + k, done[k], new)
            work[b] = new
    return jnp.concatenate(work, 0)


def factor(gram):
    n = gram.shape[0]
    row = lax.broadcasted_iota(jnp.int32, (n, n), 0)
    col = lax.broadcasted_iota(jnp.int32, (n, n), 1)
    on_diag = jnp.where(row == col, gram, 0.0)
    diag_row = jnp.sum(on_diag, 0, keepdims=True)
    down = lax.rsqrt(jnp.sum(on_diag, 1, keepdims=True))
    across = lax.rsqrt(diag_row)
    scale = jnp.where(row == col, jnp.broadcast_to(down, (n, n)), 0.0)
    work = eliminate(jnp.concatenate([gram * down * across, scale], 1), 8)
    upper = work[:, :n]
    left = lax.rsqrt(jnp.sum(jnp.where(row == col, upper, 0.0), 1, keepdims=True))
    return jnp.where(col >= row, upper * left * (diag_row * across), 0.0), work[:, n:] * left


def post(root, core_ref, mine_ref, other_ref, sketch_ref, sketch_t_ref, q_ref, proj_ref, tri_ref, gram_ref, stack):
    rank, columns = proj_ref.shape
    half = columns // 2
    blocks = half // 128
    core = core_ref[0]
    places = [pl.ds(pl.multiple_of(c * half, half), half) for c in (core, 1 - core)]
    folded = jnp.zeros((3 * rank, rank), jnp.float32)
    for i, source in enumerate((mine_ref, other_ref)):
        cross = jnp.concatenate([source[b] for b in range(blocks)], 1)
        high, mid, low = split(cross, 3)
        three = jnp.concatenate([high, mid, low], 0)
        stack[i, : 3 * rank] = three
        stack[i, 3 * rank :] = high
        folded += lax.dot_general(three, sketch_ref[:, places[i]], LAST, preferred_element_type=jnp.float32)
    folded = folded[:rank] + (folded[rank : 2 * rank] + folded[2 * rank :])
    upper, inverse = factor(0.5 * (folded + folded.T))
    tri_ref[...] = upper * (1.0 / root)
    high, low = split(inverse, 2)
    left = jnp.concatenate([high, high, high, low], 1)
    total = jnp.zeros((2 * rank, rank), jnp.float32)
    for i in range(2):
        part = jnp.dot(left, stack[i], preferred_element_type=jnp.float32)
        proj_ref[:, places[i]] = part
        pair = split(part, 2)
        total += lax.dot_general(
            jnp.concatenate(pair, 0), pair[0], LAST, preferred_element_type=jnp.float32
        )
    gram_ref[...] = (total[:rank] + (total[rank:] + total[rank:].T)) * (1.0 / columns)
    high, low = split(inverse * root, 2)
    left = jnp.concatenate([high, high, low], 1)
    s_high, s_low = split(sketch_t_ref[...], 2)
    right = jnp.concatenate([s_high, s_low, s_high], 0)
    q_ref[...] = jnp.dot(left, right, preferred_element_type=jnp.float32).astype(q_ref.dtype)


def finish(core, mine, other, sketch_matrix, sketch_t, root):
    rank, columns = sketch_matrix.shape
    vmem = pl.BlockSpec(memory_space=pltpu.VMEM)
    return pl.pallas_call(
        functools.partial(post, root),
        out_shape=(
            jax.ShapeDtypeStruct(sketch_t.shape, jnp.bfloat16),
            jax.ShapeDtypeStruct((rank, columns), jnp.float32),
            jax.ShapeDtypeStruct((rank, rank), jnp.float32),
            jax.ShapeDtypeStruct((rank, rank), jnp.float32),
        ),
        in_specs=[pl.BlockSpec(memory_space=pltpu.SMEM)] + [vmem] * 4,
        out_specs=[vmem] * 4,
        scratch_shapes=[pltpu.VMEM((2, 4 * rank, columns // 2), jnp.bfloat16)],
        compiler_params=pltpu.CompilerParams(vmem_limit_bytes=24 << 20),
        name="factor_and_project",
    )(core, mine, other, sketch_matrix, sketch_t)


def shards(slab, sketch_matrix):
    devices = lax.axis_size("rows")
    core = lax.axis_index("rows") % 2
    rank, columns = sketch_matrix.shape
    sketch_t = lax.dot_general(sketch_matrix, slab, LAST, preferred_element_type=jnp.float32)
    sketch_low = sketch_t.astype(jnp.bfloat16)
    cross_part = jnp.dot(sketch_low, slab, preferred_element_type=jnp.float32)
    blocks = columns // 128
    tiles = cross_part.reshape(rank, blocks, 128).transpose(1, 0, 2).reshape(-1, 8, 128)
    halves = [half.reshape(blocks // 2, rank, 128) for half in all_reduce(tiles, core)]
    return finish(core.reshape(1), *halves, sketch_matrix, sketch_t, math.sqrt(slab.shape[0] * devices))


def solution(mesh):
    return jax.shard_map(
        shards,
        mesh=mesh,
        in_specs=(P("rows", None), P()),
        out_specs=(P(None, "rows"), P(), P(), P()),
        check_vma=False,
    )
```

```python
import functools
import math

import jax
import jax.numpy as jnp
from jax import lax
from jax.experimental import pallas as pl
from jax.experimental.pallas import tpu as pltpu
from jax.sharding import PartitionSpec as P

SIZES = dict(z=8, y=8, x=4, c=2)


def place(index):
    coords = {}
    for name in reversed(SIZES):
        index, coords[name] = divmod(index, SIZES[name])
    return coords


def groups(axes_of_core):
    out = {}
    for index in range(math.prod(SIZES.values())):
        coords = place(index)
        axes = axes_of_core[coords["c"]]
        key = (coords["c"],) + tuple(value for name, value in coords.items() if name not in axes)
        out.setdefault(key, []).append(index)
    return list(out.values())


PLANE = groups(("yx", "zx"))
LINE = groups(("z", "y"))
PAIRS = [(i, i ^ 1) for i in range(math.prod(SIZES.values()))]


def exchange(pieces, peers):
    return lax.all_to_all(pieces, "rows", 0, 0, axis_index_groups=peers, tiled=True)


def summed(tiles, count):
    return tiles.reshape(count, tiles.shape[0] // count, 8, 128).sum(0)


def spread(tiles, peers):
    return exchange(jnp.tile(tiles, (len(peers[0]), 1, 1)), peers)


def all_reduce(give, keep):
    part = keep + lax.ppermute(give, "rows", PAIRS)
    part = summed(exchange(part, PLANE), len(PLANE[0]))
    part = summed(spread(part, LINE), len(LINE[0]))
    mine = spread(part, PLANE)
    return mine, lax.ppermute(mine, "rows", PAIRS)


LAST = (((1,), (1,)), ((), ()))


def split(value, parts):
    out = []
    for _ in range(parts):
        out.append(value.astype(jnp.bfloat16))
        value = value - out[-1].astype(jnp.float32)
    return out


def eliminate(work, size):
    sub = lax.broadcasted_iota(jnp.int32, (8, 128), 0)

    def row(tile, k):
        return jnp.broadcast_to(tile[k : k + 1, :], (8, 128))

    work = [work[8 * b : 8 * b + 8] for b in range(work.shape[0] // 8)]
    for first in range(0, 8 * len(work), size):
        top, at = divmod(first, 8)
        live = range(top, len(work))
        column = [
            {b: jnp.broadcast_to(work[b][:, first + k : first + k + 1], (8, 128)) for b in live}
            for k in range(size)
        ]
        pivot = [row(work[top], at + k) for k in range(size)]
        m = {(i, k): row(column[k][top], at + i) for k in range(size) for i in range(k, size)}
        x, done, scaled = {}, {}, {}
        for k in range(0, size, 2):
            a, b, d = m[k, k], m[k + 1, k], m[k + 1, k + 1]
            inverse = 1.0 / (a * d - b * b)
            ai, bi, di = a * inverse, b * inverse, d * inverse
            rest = range(k + 2, size)
            for i in rest:
                x[i, k] = di * m[i, k] - bi * m[i, k + 1]
                x[i, k + 1] = ai * m[i, k + 1] - bi * m[i, k]
            for i in rest:
                for j in range(k + 2, i + 1):
                    m[i, j] = m[i, j] - x[i, k] * m[j, k] - x[i, k + 1] * m[j, k + 1]
            done[k] = pivot[k]
            done[k + 1] = pivot[k + 1] - (b * (1.0 / a)) * pivot[k]
            scaled[k] = di * pivot[k] - bi * pivot[k + 1]
            scaled[k + 1] = ai * pivot[k + 1] - bi * pivot[k]
            for i in rest:
                pivot[i] = pivot[i] - x[i, k] * pivot[k] - x[i, k + 1] * pivot[k + 1]
        for k in reversed(range(size)):
            for i in range(k // 2 * 2 + 2, size):
                scaled[k] = scaled[k] - x[i, k] * scaled[i]
        for b in live:
            new = work[b]
            if b > top or at + size < 8:
                terms = [column[k][b] * scaled[k] for k in range(size)]
                while len(terms) > 1:
                    terms = [terms[i] + terms[i + 1] for i in range(0, len(terms), 2)]
                new = new - terms[0]
            if b == top:
                new = jnp.where(sub >= at + size, new, work[b])
                for k in range(1, size):
                    new = jnp.where(sub == at + k, done[k], new)
            work[b] = new
    return jnp.concatenate(work, 0)


def factor(gram):
    n = gram.shape[0]
    row = lax.broadcasted_iota(jnp.int32, (n, n), 0)
    col = lax.broadcasted_iota(jnp.int32, (n, n), 1)
    on_diag = jnp.where(row == col, gram, 0.0)
    diag_row = jnp.sum(on_diag, 0, keepdims=True)
    down = lax.rsqrt(jnp.sum(on_diag, 1, keepdims=True))
    across = lax.rsqrt(diag_row)
    scale = jnp.where(row == col, jnp.broadcast_to(down, (n, n)), 0.0)
    work = eliminate(jnp.concatenate([gram * down * across, scale], 1), 8)
    upper = work[:, :n]
    left = lax.rsqrt(jnp.sum(jnp.where(row == col, upper, 0.0), 1, keepdims=True))
    return jnp.where(col >= row, upper * left * (diag_row * across), 0.0), work[:, n:] * left


def pre(core_ref, slab_hbm, sketch_hbm, sketch_t_ref, give_ref, keep_ref, slab_ref, sketch_ref, arrived):
    columns = slab_ref.shape[1]
    chunks = arrived.shape[1]
    width = columns // chunks
    views = [pl.ds(i * width, width) for i in range(chunks)]
    copies = [
        [
            pltpu.make_async_copy(source.at[:, view], target.at[:, view], arrived.at[j, i])
            for j, (source, target) in enumerate(((sketch_hbm, sketch_ref), (slab_hbm, slab_ref)))
        ]
        for i, view in enumerate(views)
    ]
    for pair in copies:
        for copy in pair:
            copy.start()
    sketch_t = jnp.zeros(sketch_t_ref.shape, jnp.float32)
    for pair, view in zip(copies, views):
        for copy in pair:
            copy.wait()
        sketch_t += lax.dot_general(
            sketch_ref[:, view], slab_ref[:, view], LAST, preferred_element_type=jnp.float32
        )
    sketch_t_ref[...] = sketch_t
    sketch_low = sketch_t.astype(jnp.bfloat16)
    core = core_ref[0]
    half = columns // 2
    for c, out_ref in ((1 - core, give_ref), (core, keep_ref)):
        view = pl.ds(pl.multiple_of(c * half, half), half)
        part = jnp.dot(sketch_low, slab_ref[:, view], preferred_element_type=jnp.float32)
        for b in range(half // 128):
            out_ref[b] = part[:, b * 128 : (b + 1) * 128]


def begin(core, slab, sketch_matrix, chunks=4):
    rows, columns = slab.shape
    rank = sketch_matrix.shape[0]
    vmem = pl.BlockSpec(memory_space=pltpu.VMEM)
    hbm = pl.BlockSpec(memory_space=pltpu.HBM)
    slab, sketch_matrix = (pltpu.with_memory_space_constraint(a, pltpu.HBM) for a in (slab, sketch_matrix))
    half = pltpu.VMEM((columns // 256, rank, 128), jnp.float32)
    return pl.pallas_call(
        pre,
        out_shape=(pltpu.VMEM((rank, rows), jnp.float32), half, half),
        in_specs=[pl.BlockSpec(memory_space=pltpu.SMEM), hbm, hbm],
        out_specs=[vmem] * 3,
        scratch_shapes=[
            pltpu.VMEM(slab.shape, slab.dtype),
            pltpu.VMEM(sketch_matrix.shape, sketch_matrix.dtype),
            pltpu.SemaphoreType.DMA((2, chunks)),
        ],
        compiler_params=pltpu.CompilerParams(vmem_limit_bytes=16 << 20),
        name="sketch_and_cross",
    )(core, slab, sketch_matrix)


def post(root, core_ref, mine_ref, other_ref, sketch_ref, sketch_t_ref, q_ref, proj_ref, tri_ref, gram_ref, stack):
    rank, columns = proj_ref.shape
    half = columns // 2
    blocks = half // 128
    core = core_ref[0]
    places = [pl.ds(pl.multiple_of(c * half, half), half) for c in (core, 1 - core)]
    folded = jnp.zeros((3 * rank, rank), jnp.float32)
    for i, source in enumerate((mine_ref, other_ref)):
        cross = jnp.concatenate([source[b] for b in range(blocks)], 1)
        high, mid, low = split(cross, 3)
        three = jnp.concatenate([high, mid, low], 0)
        stack[i, : 3 * rank] = three
        stack[i, 3 * rank :] = high
        folded += lax.dot_general(three, sketch_ref[:, places[i]], LAST, preferred_element_type=jnp.float32)
    folded = folded[:rank] + (folded[rank : 2 * rank] + folded[2 * rank :])
    upper, inverse = factor(0.5 * (folded + folded.T))
    tri_ref[...] = upper * (1.0 / root)
    high, low = split(inverse, 2)
    left = jnp.concatenate([high, high, high, low], 1)
    total = jnp.zeros((2 * rank, rank), jnp.float32)
    for i in range(2):
        part = jnp.dot(left, stack[i], preferred_element_type=jnp.float32)
        proj_ref[:, places[i]] = part
        pair = split(part, 2)
        total += lax.dot_general(
            jnp.concatenate(pair, 0), pair[0], LAST, preferred_element_type=jnp.float32
        )
    gram_ref[...] = (total[:rank] + (total[rank:] + total[rank:].T)) * (1.0 / columns)
    high, low = split(inverse * root, 2)
    left = jnp.concatenate([high, high, low], 1)
    s_high, s_low = split(sketch_t_ref[...], 2)
    right = jnp.concatenate([s_high, s_low, s_high], 0)
    q_ref[...] = jnp.dot(left, right, preferred_element_type=jnp.float32).astype(q_ref.dtype)


def finish(core, mine, other, sketch_matrix, sketch_t, root):
    rank, columns = sketch_matrix.shape
    vmem = pl.BlockSpec(memory_space=pltpu.VMEM)
    return pl.pallas_call(
        functools.partial(post, root),
        out_shape=(
            jax.ShapeDtypeStruct(sketch_t.shape, jnp.bfloat16),
            jax.ShapeDtypeStruct((rank, columns), jnp.float32),
            jax.ShapeDtypeStruct((rank, rank), jnp.float32),
            jax.ShapeDtypeStruct((rank, rank), jnp.float32),
        ),
        in_specs=[pl.BlockSpec(memory_space=pltpu.SMEM)] + [vmem] * 4,
        out_specs=[vmem] * 4,
        scratch_shapes=[pltpu.VMEM((2, 4 * rank, columns // 2), jnp.bfloat16)],
        compiler_params=pltpu.CompilerParams(vmem_limit_bytes=24 << 20),
        name="factor_and_project",
    )(core, mine, other, sketch_matrix, sketch_t)


def shards(slab, sketch_matrix):
    devices = lax.axis_size("rows")
    core = (lax.axis_index("rows") % 2).reshape(1)
    sketch_t, give, keep = begin(core, slab, sketch_matrix)
    shape = give.shape
    halves = all_reduce(give.reshape(-1, 8, 128), keep.reshape(-1, 8, 128))
    mine, other = (half.reshape(shape) for half in halves)
    return finish(core, mine, other, sketch_matrix, sketch_t, math.sqrt(slab.shape[0] * devices))


def solution(mesh):
    return jax.shard_map(
        shards,
        mesh=mesh,
        in_specs=(P("rows", None), P()),
        out_specs=(P(None, "rows"), P(), P(), P()),
        check_vma=False,
    )
```

```python
import functools
import math

import jax
import jax.numpy as jnp
from jax import lax
from jax.experimental import pallas as pl
from jax.experimental.pallas import tpu as pltpu
from jax.sharding import PartitionSpec as P

SIZES = dict(z=8, y=8, x=4, c=2)


def place(index):
    coords = {}
    for name in reversed(SIZES):
        index, coords[name] = divmod(index, SIZES[name])
    return coords


def groups(axes_of_core):
    out = {}
    for index in range(math.prod(SIZES.values())):
        coords = place(index)
        axes = axes_of_core[coords["c"]]
        key = (coords["c"],) + tuple(value for name, value in coords.items() if name not in axes)
        out.setdefault(key, []).append(index)
    return list(out.values())


PLANE = groups(("yx", "zx"))
LINE = groups(("z", "y"))
PAIRS = [(i, i ^ 1) for i in range(math.prod(SIZES.values()))]


def exchange(pieces, peers):
    return lax.all_to_all(pieces, "rows", 0, 0, axis_index_groups=peers, tiled=True)


def summed(tiles, count):
    return tiles.reshape(count, tiles.shape[0] // count, 8, 128).sum(0)


def spread(tiles, peers):
    return exchange(jnp.tile(tiles, (len(peers[0]), 1, 1)), peers)


def all_reduce(part):
    part = summed(exchange(part, PLANE), len(PLANE[0]))
    part = summed(spread(part, LINE), len(LINE[0]))
    return spread(part, PLANE)


LAST = (((1,), (1,)), ((), ()))


def split(value, parts):
    out = []
    for _ in range(parts):
        out.append(value.astype(jnp.bfloat16))
        value = value - out[-1].astype(jnp.float32)
    return out


def eliminate(work, size):
    sub = lax.broadcasted_iota(jnp.int32, (8, 128), 0)

    def row(tile, k):
        return jnp.broadcast_to(tile[k : k + 1, :], (8, 128))

    work = [work[8 * b : 8 * b + 8] for b in range(work.shape[0] // 8)]
    for first in range(0, 8 * len(work), size):
        top, at = divmod(first, 8)
        live = range(top, len(work))
        column = [
            {b: jnp.broadcast_to(work[b][:, first + k : first + k + 1], (8, 128)) for b in live}
            for k in range(size)
        ]
        pivot = [row(work[top], at + k) for k in range(size)]
        m = {(i, k): row(column[k][top], at + i) for k in range(size) for i in range(k, size)}
        x, done, scaled = {}, {}, {}
        for k in range(0, size, 2):
            a, b, d = m[k, k], m[k + 1, k], m[k + 1, k + 1]
            inverse = 1.0 / (a * d - b * b)
            ai, bi, di = a * inverse, b * inverse, d * inverse
            rest = range(k + 2, size)
            for i in rest:
                x[i, k] = di * m[i, k] - bi * m[i, k + 1]
                x[i, k + 1] = ai * m[i, k + 1] - bi * m[i, k]
            for i in rest:
                for j in range(k + 2, i + 1):
                    m[i, j] = m[i, j] - x[i, k] * m[j, k] - x[i, k + 1] * m[j, k + 1]
            done[k] = pivot[k]
            done[k + 1] = pivot[k + 1] - (b * (1.0 / a)) * pivot[k]
            scaled[k] = di * pivot[k] - bi * pivot[k + 1]
            scaled[k + 1] = ai * pivot[k + 1] - bi * pivot[k]
            for i in rest:
                pivot[i] = pivot[i] - x[i, k] * pivot[k] - x[i, k + 1] * pivot[k + 1]
        for k in reversed(range(size)):
            for i in range(k // 2 * 2 + 2, size):
                scaled[k] = scaled[k] - x[i, k] * scaled[i]
        for b in live:
            new = work[b]
            if b > top or at + size < 8:
                terms = [column[k][b] * scaled[k] for k in range(size)]
                while len(terms) > 1:
                    terms = [terms[i] + terms[i + 1] for i in range(0, len(terms), 2)]
                new = new - terms[0]
            if b == top:
                new = jnp.where(sub >= at + size, new, work[b])
                for k in range(1, size):
                    new = jnp.where(sub == at + k, done[k], new)
            work[b] = new
    return jnp.concatenate(work, 0)


def factor(gram):
    n = gram.shape[0]
    row = lax.broadcasted_iota(jnp.int32, (n, n), 0)
    col = lax.broadcasted_iota(jnp.int32, (n, n), 1)
    on_diag = jnp.where(row == col, gram, 0.0)
    diag_row = jnp.sum(on_diag, 0, keepdims=True)
    down = lax.rsqrt(jnp.sum(on_diag, 1, keepdims=True))
    across = lax.rsqrt(diag_row)
    scale = jnp.where(row == col, jnp.broadcast_to(down, (n, n)), 0.0)
    work = eliminate(jnp.concatenate([gram * down * across, scale], 1), 8)
    upper = work[:, :n]
    left = lax.rsqrt(jnp.sum(jnp.where(row == col, upper, 0.0), 1, keepdims=True))
    return jnp.where(col >= row, upper * left * (diag_row * across), 0.0), work[:, n:] * left


def pre(core_ref, slab_hbm, sketch_hbm, sketch_t_ref, slab_ref, give_ref, sketch_ref, arrived):
    columns = slab_ref.shape[1]
    chunks = arrived.shape[1]
    width = columns // chunks
    views = [pl.ds(i * width, width) for i in range(chunks)]
    copies = [
        [
            pltpu.make_async_copy(source.at[:, view], target.at[:, view], arrived.at[j, i])
            for j, (source, target) in enumerate(((sketch_hbm, sketch_ref), (slab_hbm, slab_ref)))
        ]
        for i, view in enumerate(views)
    ]
    for pair in copies:
        for copy in pair:
            copy.start()
    sketch_t = jnp.zeros(sketch_t_ref.shape, jnp.float32)
    for pair, view in zip(copies, views):
        for copy in pair:
            copy.wait()
        sketch_t += lax.dot_general(
            sketch_ref[:, view], slab_ref[:, view], LAST, preferred_element_type=jnp.float32
        )
    sketch_t_ref[...] = sketch_t
    cross_half(1 - core_ref[0], sketch_t, slab_ref, give_ref)


def cross_half(which, sketch_t, slab_ref, out_ref):
    half = slab_ref.shape[1] // 2
    view = pl.ds(pl.multiple_of(which * half, half), half)
    part = jnp.dot(sketch_t.astype(jnp.bfloat16), slab_ref[:, view], preferred_element_type=jnp.float32)
    for b in range(half // 128):
        out_ref[b] = part[:, b * 128 : (b + 1) * 128]


def pre_keep(core_ref, sketch_t_ref, slab_ref, keep_ref):
    cross_half(core_ref[0], sketch_t_ref[...], slab_ref, keep_ref)


SCALAR = pl.BlockSpec(memory_space=pltpu.SMEM)
VMEM = pl.BlockSpec(memory_space=pltpu.VMEM)
LIMIT = pltpu.CompilerParams(vmem_limit_bytes=16 << 20)


def begin(core, slab, sketch_matrix, chunks=4):
    rows, columns = slab.shape
    rank = sketch_matrix.shape[0]
    slab, sketch_matrix = (pltpu.with_memory_space_constraint(a, pltpu.HBM) for a in (slab, sketch_matrix))
    hbm = pl.BlockSpec(memory_space=pltpu.HBM)
    return pl.pallas_call(
        pre,
        out_shape=(
            pltpu.VMEM((rank, rows), jnp.float32),
            pltpu.VMEM(slab.shape, slab.dtype),
            pltpu.VMEM((columns // 256, rank, 128), jnp.float32),
        ),
        in_specs=[SCALAR, hbm, hbm],
        out_specs=[VMEM] * 3,
        scratch_shapes=[
            pltpu.VMEM(sketch_matrix.shape, sketch_matrix.dtype),
            pltpu.SemaphoreType.DMA((2, chunks)),
        ],
        compiler_params=LIMIT,
        name="sketch_and_cross_to_give",
    )(core, slab, sketch_matrix)


def keep_half(core, sketch_t, slab):
    rows, columns = slab.shape
    rank = sketch_t.shape[0]
    return pl.pallas_call(
        pre_keep,
        out_shape=pltpu.VMEM((columns // 256, rank, 128), jnp.float32),
        in_specs=[SCALAR, VMEM, VMEM],
        out_specs=VMEM,
        compiler_params=LIMIT,
        cost_estimate=pl.CostEstimate(flops=rank * rows * columns, bytes_accessed=slab.size, transcendentals=0),
        name="cross_to_keep",
    )(core, sketch_t, slab)


def fold_half(which, source, sketch_ref, stack):
    rank = sketch_ref.shape[0]
    half = source.shape[0] * 128
    cross = jnp.concatenate([source[b] for b in range(source.shape[0])], 1)
    high, mid, low = split(cross, 3)
    stack[...] = jnp.concatenate([high, mid, low, high], 0)
    view = pl.ds(pl.multiple_of(which * half, half), half)
    out = lax.dot_general(stack[: 3 * rank], sketch_ref[:, view], LAST, preferred_element_type=jnp.float32)
    return out[:rank] + (out[rank : 2 * rank] + out[2 * rank :])


def post_mine(core_ref, mine_ref, sketch_ref, stack, folded_ref):
    folded_ref[...] = fold_half(core_ref[0], mine_ref, sketch_ref, stack)


def fold_mine(core, mine, sketch_matrix):
    rank, columns = sketch_matrix.shape
    return pl.pallas_call(
        post_mine,
        out_shape=(
            pltpu.VMEM((4 * rank, columns // 2), jnp.bfloat16),
            pltpu.VMEM((rank, rank), jnp.float32),
        ),
        in_specs=[SCALAR, VMEM, VMEM],
        out_specs=[VMEM] * 2,
        compiler_params=LIMIT,
        cost_estimate=pl.CostEstimate(
            flops=3 * rank * rank * columns, bytes_accessed=4 * rank * columns, transcendentals=0
        ),
        name="fold_mine",
    )(core, mine, sketch_matrix)


def post(
    root, core_ref, mine_stack, folded_ref, other_ref, sketch_ref, sketch_t_ref, q_ref, proj_ref, tri_ref, gram_ref, other_stack
):
    rank, columns = proj_ref.shape
    half = columns // 2
    core = core_ref[0]
    folded = folded_ref[...] + fold_half(1 - core, other_ref, sketch_ref, other_stack)
    upper, inverse = factor(0.5 * (folded + folded.T))
    tri_ref[...] = upper * (1.0 / root)
    high, low = split(inverse, 2)
    left = jnp.concatenate([high, high, high, low], 1)
    total = jnp.zeros((2 * rank, rank), jnp.float32)
    for which, stack in ((core, mine_stack), (1 - core, other_stack)):
        part = jnp.dot(left, stack[...], preferred_element_type=jnp.float32)
        proj_ref[:, pl.ds(pl.multiple_of(which * half, half), half)] = part
        pair = split(part, 2)
        total += lax.dot_general(
            jnp.concatenate(pair, 0), pair[0], LAST, preferred_element_type=jnp.float32
        )
    gram_ref[...] = (total[:rank] + (total[rank:] + total[rank:].T)) * (1.0 / columns)
    high, low = split(inverse * root, 2)
    left = jnp.concatenate([high, high, low], 1)
    s_high, s_low = split(sketch_t_ref[...], 2)
    right = jnp.concatenate([s_high, s_low, s_high], 0)
    q_ref[...] = jnp.dot(left, right, preferred_element_type=jnp.float32).astype(q_ref.dtype)


def finish(core, mine_stack, folded, other, sketch_matrix, sketch_t, root):
    rank, columns = sketch_matrix.shape
    return pl.pallas_call(
        functools.partial(post, root),
        out_shape=(
            jax.ShapeDtypeStruct(sketch_t.shape, jnp.bfloat16),
            jax.ShapeDtypeStruct((rank, columns), jnp.float32),
            jax.ShapeDtypeStruct((rank, rank), jnp.float32),
            jax.ShapeDtypeStruct((rank, rank), jnp.float32),
        ),
        in_specs=[SCALAR] + [VMEM] * 5,
        out_specs=[VMEM] * 4,
        scratch_shapes=[pltpu.VMEM((4 * rank, columns // 2), jnp.bfloat16)],
        compiler_params=pltpu.CompilerParams(vmem_limit_bytes=24 << 20),
        name="factor_and_project",
    )(core, mine_stack, folded, other, sketch_matrix, sketch_t)


def shards(slab, sketch_matrix):
    devices = lax.axis_size("rows")
    core = (lax.axis_index("rows") % 2).reshape(1)
    sketch_t, slab_near, give = begin(core, slab, sketch_matrix)
    shape = give.shape
    got = lax.ppermute(give, "rows", PAIRS)
    keep = keep_half(core, sketch_t, slab_near)
    mine = all_reduce((keep + got).reshape(-1, 8, 128)).reshape(shape)
    other = lax.ppermute(mine, "rows", PAIRS)
    stack, folded = fold_mine(core, mine, sketch_matrix)
    return finish(core, stack, folded, other, sketch_matrix, sketch_t, math.sqrt(slab.shape[0] * devices))


def solution(mesh):
    return jax.shard_map(
        shards,
        mesh=mesh,
        in_specs=(P("rows", None), P()),
        out_specs=(P(None, "rows"), P(), P(), P()),
        check_vma=False,
    )
```

```python
import functools
import math

import jax
import jax.numpy as jnp
from jax import lax
from jax.experimental import pallas as pl
from jax.experimental.pallas import tpu as pltpu
from jax.sharding import PartitionSpec as P

SIZES = dict(z=8, y=8, x=4, c=2)


def place(index):
    coords = {}
    for name in reversed(SIZES):
        index, coords[name] = divmod(index, SIZES[name])
    return coords


def groups(axes_of_core):
    out = {}
    for index in range(math.prod(SIZES.values())):
        coords = place(index)
        axes = axes_of_core[coords["c"]]
        key = (coords["c"],) + tuple(value for name, value in coords.items() if name not in axes)
        out.setdefault(key, []).append(index)
    return list(out.values())


PLANE = groups(("yx", "zx"))
LINE = groups(("z", "y"))
PAIRS = [(i, i ^ 1) for i in range(math.prod(SIZES.values()))]


def exchange(pieces, peers):
    return lax.all_to_all(pieces, "rows", 0, 0, axis_index_groups=peers, tiled=True)


def summed(tiles, count):
    return tiles.reshape(count, tiles.shape[0] // count, 8, 128).sum(0)


def spread(tiles, peers):
    return exchange(jnp.tile(tiles, (len(peers[0]), 1, 1)), peers)


def all_reduce(part):
    part = summed(exchange(part, PLANE), len(PLANE[0]))
    part = summed(spread(part, LINE), len(LINE[0]))
    return spread(part, PLANE)


LAST = (((1,), (1,)), ((), ()))


def split(value, parts):
    out = []
    for _ in range(parts):
        out.append(value.astype(jnp.bfloat16))
        value = value - out[-1].astype(jnp.float32)
    return out


def eliminate(work, size, base):
    sub = lax.broadcasted_iota(jnp.int32, (8, 128), 0)

    def row(tile, k):
        return jnp.broadcast_to(tile[k : k + 1, :], (8, 128))

    work = [work[8 * b : 8 * b + 8] for b in range(work.shape[0] // 8)]
    for first in range(0, 8 * len(work), size):
        top, at = divmod(first, 8)
        live = range(top, len(work))
        column = [
            {b: jnp.broadcast_to(work[b][:, base + first + k : base + first + k + 1], (8, 128)) for b in live}
            for k in range(size)
        ]
        pivot = [row(work[top], at + k) for k in range(size)]
        m = {(i, k): row(column[k][top], at + i) for k in range(size) for i in range(k, size)}
        x, done, scaled = {}, {}, {}
        for k in range(0, size, 2):
            a, b, d = m[k, k], m[k + 1, k], m[k + 1, k + 1]
            if k % 4 == 0:
                det = a * d - b * b
                y = {i: (d * m[i, k] - b * m[i, k + 1], a * m[i, k + 1] - b * m[i, k]) for i in (k + 2, k + 3)}
                e, f, g = (
                    det * m[i, j] - (y[i][0] * m[j, k] + y[i][1] * m[j, k + 1])
                    for i, j in ((k + 2, k + 2), (k + 3, k + 2), (k + 3, k + 3))
                )
                after = det * (1.0 / (e * g - f * f))
                inverse = 1.0 / det
                ai, bi, di = a * inverse, b * inverse, d * inverse
            else:
                ai, bi, di = e * after, f * after, g * after
            rest = range(k + 2, size)
            for i in rest:
                x[i, k] = di * m[i, k] - bi * m[i, k + 1]
                x[i, k + 1] = ai * m[i, k + 1] - bi * m[i, k]
            for i in rest:
                for j in range(k + 2, i + 1):
                    m[i, j] = m[i, j] - x[i, k] * m[j, k] - x[i, k + 1] * m[j, k + 1]
            done[k] = pivot[k]
            done[k + 1] = pivot[k + 1] - (b * (1.0 / a)) * pivot[k]
            scaled[k] = di * pivot[k] - bi * pivot[k + 1]
            scaled[k + 1] = ai * pivot[k + 1] - bi * pivot[k]
            for i in rest:
                pivot[i] = pivot[i] - x[i, k] * pivot[k] - x[i, k + 1] * pivot[k + 1]
        for k in reversed(range(size)):
            for i in range(k // 2 * 2 + 2, size):
                scaled[k] = scaled[k] - x[i, k] * scaled[i]
        for b in live:
            new = work[b]
            if b > top or at + size < 8:
                terms = [column[k][b] * scaled[k] for k in range(size)]
                while len(terms) > 1:
                    terms = [terms[i] + terms[i + 1] for i in range(0, len(terms), 2)]
                new = new - terms[0]
            if b == top:
                new = jnp.where(sub >= at + size, new, work[b])
                for k in range(1, size):
                    new = jnp.where(sub == at + k, done[k], new)
            work[b] = new
    return jnp.concatenate(work, 0)


def factor(gram):
    n = gram.shape[0]
    row = lax.broadcasted_iota(jnp.int32, (n, n), 0)
    col = lax.broadcasted_iota(jnp.int32, (n, n), 1)
    on_diag = jnp.where(row == col, gram, 0.0)
    diag_row = jnp.sum(on_diag, 0, keepdims=True)
    down = lax.rsqrt(jnp.sum(on_diag, 1, keepdims=True))
    across = lax.rsqrt(diag_row)
    scale = jnp.where(row == col, jnp.broadcast_to(down, (n, n)), 0.0)
    work = jnp.concatenate([gram * down * across, scale], 1)
    top = eliminate(work[: n // 2], 8, 0)
    pivots = jnp.sum(jnp.where((row == col)[: n // 2], top[:, :n], 0.0), 1, keepdims=True)
    h, m, l = split((top * (1.0 / pivots)).T[n // 2 : n], 3)
    th, tm, tl = split(top, 3)
    share = jnp.dot(
        jnp.concatenate([h, h, m, h, m, l], 1),
        jnp.concatenate([th, tm, th, tl, tm, th], 0),
        preferred_element_type=jnp.float32,
    )
    low = eliminate(work[n // 2 :] - share, 8, n // 2)
    work = jnp.concatenate([top, low], 0)
    upper = work[:, :n]
    left = lax.rsqrt(jnp.sum(jnp.where(row == col, upper, 0.0), 1, keepdims=True))
    return jnp.where(col >= row, upper * left * (diag_row * across), 0.0), work[:, n:] * left


def pre(widths, core_ref, slab_hbm, sketch_hbm, sketch_t_ref, slab_ref, give_ref, sketch_ref, arrived):
    views, at = [], 0
    for width in widths:
        views.append(pl.ds(at, width))
        at += width
    copies = [
        [
            pltpu.make_async_copy(source.at[:, view], target.at[:, view], arrived.at[j, i])
            for j, (source, target) in enumerate(((sketch_hbm, sketch_ref), (slab_hbm, slab_ref)))
        ]
        for i, view in enumerate(views)
    ]
    for pair in copies:
        for copy in pair:
            copy.start()
    sketch_t = jnp.zeros(sketch_t_ref.shape, jnp.float32)
    for pair, view in zip(copies, views):
        for copy in pair:
            copy.wait()
        sketch_t += lax.dot_general(
            sketch_ref[:, view], slab_ref[:, view], LAST, preferred_element_type=jnp.float32
        )
    sketch_t_ref[...] = sketch_t
    cross_half(1 - core_ref[0], sketch_t, slab_ref, give_ref)


def cross_half(which, sketch_t, slab_ref, out_ref):
    half = slab_ref.shape[1] // 2
    view = pl.ds(pl.multiple_of(which * half, half), half)
    part = jnp.dot(sketch_t.astype(jnp.bfloat16), slab_ref[:, view], preferred_element_type=jnp.float32)
    for b in range(half // 128):
        out_ref[b] = part[:, b * 128 : (b + 1) * 128]


def pre_keep(core_ref, sketch_t_ref, slab_ref, keep_ref):
    cross_half(core_ref[0], sketch_t_ref[...], slab_ref, keep_ref)


SCALAR = pl.BlockSpec(memory_space=pltpu.SMEM)
VMEM = pl.BlockSpec(memory_space=pltpu.VMEM)
LIMIT = pltpu.CompilerParams(vmem_limit_bytes=16 << 20)


def begin(core, slab, sketch_matrix):
    rows, columns = slab.shape
    widths = [columns * part // 16 for part in (1, 3, 5, 7)]
    rank = sketch_matrix.shape[0]
    slab, sketch_matrix = (pltpu.with_memory_space_constraint(a, pltpu.HBM) for a in (slab, sketch_matrix))
    hbm = pl.BlockSpec(memory_space=pltpu.HBM)
    return pl.pallas_call(
        functools.partial(pre, widths),
        out_shape=(
            pltpu.VMEM((rank, rows), jnp.float32),
            pltpu.VMEM(slab.shape, slab.dtype),
            pltpu.VMEM((columns // 256, rank, 128), jnp.float32),
        ),
        in_specs=[SCALAR, hbm, hbm],
        out_specs=[VMEM] * 3,
        scratch_shapes=[
            pltpu.VMEM(sketch_matrix.shape, sketch_matrix.dtype),
            pltpu.SemaphoreType.DMA((2, len(widths))),
        ],
        compiler_params=LIMIT,
        name="sketch_and_cross_to_give",
    )(core, slab, sketch_matrix)


def keep_half(core, sketch_t, slab):
    rows, columns = slab.shape
    rank = sketch_t.shape[0]
    return pl.pallas_call(
        pre_keep,
        out_shape=pltpu.VMEM((columns // 256, rank, 128), jnp.float32),
        in_specs=[SCALAR, VMEM, VMEM],
        out_specs=VMEM,
        compiler_params=LIMIT,
        cost_estimate=pl.CostEstimate(flops=rank * rows * columns, bytes_accessed=slab.size, transcendentals=0),
        name="cross_to_keep",
    )(core, sketch_t, slab)


def fold_half(which, source, sketch_ref, stack):
    rank = sketch_ref.shape[0]
    half = source.shape[0] * 128
    cross = jnp.concatenate([source[b] for b in range(source.shape[0])], 1)
    high, mid, low = split(cross, 3)
    stack[...] = jnp.concatenate([high, mid], 0)
    view = pl.ds(pl.multiple_of(which * half, half), half)
    three = jnp.concatenate([high, mid, low], 0)
    out = lax.dot_general(three, sketch_ref[:, view], LAST, preferred_element_type=jnp.float32)
    return out[:rank] + (out[rank : 2 * rank] + out[2 * rank :])


def post_mine(core_ref, mine_ref, sketch_ref, stack, folded_ref):
    folded_ref[...] = fold_half(core_ref[0], mine_ref, sketch_ref, stack)


def fold_mine(core, mine, sketch_matrix):
    rank, columns = sketch_matrix.shape
    return pl.pallas_call(
        post_mine,
        out_shape=(
            pltpu.VMEM((2 * rank, columns // 2), jnp.bfloat16),
            pltpu.VMEM((rank, rank), jnp.float32),
        ),
        in_specs=[SCALAR, VMEM, VMEM],
        out_specs=[VMEM] * 2,
        compiler_params=LIMIT,
        cost_estimate=pl.CostEstimate(
            flops=3 * rank * rank * columns, bytes_accessed=4 * rank * columns, transcendentals=0
        ),
        name="fold_mine",
    )(core, mine, sketch_matrix)


def post(
    root, core_ref, mine_stack, folded_ref, other_ref, sketch_ref, sketch_t_ref, q_ref, proj_ref, tri_ref, gram_ref, other_stack
):
    rank, columns = proj_ref.shape
    half = columns // 2
    core = core_ref[0]
    folded = folded_ref[...] + fold_half(1 - core, other_ref, sketch_ref, other_stack)
    upper, inverse = factor(0.5 * (folded + folded.T))
    tri_ref[...] = upper * (1.0 / root)
    high, low = split(inverse, 2)
    left = jnp.concatenate(
        [jnp.concatenate([high, high], 1), jnp.concatenate([low, jnp.zeros_like(low)], 1)], 0
    )
    total = jnp.zeros((2 * rank, rank), jnp.float32)
    for which, stack in ((core, mine_stack), (1 - core, other_stack)):
        for at in range(0, half, 512):
            part = jnp.dot(left, stack[:, at : at + 512], preferred_element_type=jnp.float32)
            part = part[:rank] + part[rank:]
            proj_ref[:, pl.ds(pl.multiple_of(which * half + at, 128), 512)] = part
            pair = split(part, 2)
            total += lax.dot_general(
                jnp.concatenate(pair, 0), pair[0], LAST, preferred_element_type=jnp.float32
            )
    gram_ref[...] = (total[:rank] + (total[rank:] + total[rank:].T)) * (1.0 / columns)
    high, low = split(inverse * root, 2)
    left = jnp.concatenate([high, high, low], 1)
    s_high, s_low = split(sketch_t_ref[...], 2)
    right = jnp.concatenate([s_high, s_low, s_high], 0)
    q_ref[...] = jnp.dot(left, right, preferred_element_type=jnp.float32).astype(q_ref.dtype)


def finish(core, mine_stack, folded, other, sketch_matrix, sketch_t, root):
    rank, columns = sketch_matrix.shape
    return pl.pallas_call(
        functools.partial(post, root),
        out_shape=(
            jax.ShapeDtypeStruct(sketch_t.shape, jnp.bfloat16),
            jax.ShapeDtypeStruct((rank, columns), jnp.float32),
            jax.ShapeDtypeStruct((rank, rank), jnp.float32),
            jax.ShapeDtypeStruct((rank, rank), jnp.float32),
        ),
        in_specs=[SCALAR] + [VMEM] * 5,
        out_specs=[VMEM] * 4,
        scratch_shapes=[pltpu.VMEM((2 * rank, columns // 2), jnp.bfloat16)],
        compiler_params=pltpu.CompilerParams(vmem_limit_bytes=24 << 20),
        name="factor_and_project",
    )(core, mine_stack, folded, other, sketch_matrix, sketch_t)


def shards(slab, sketch_matrix):
    devices = lax.axis_size("rows")
    core = (lax.axis_index("rows") % 2).reshape(1)
    sketch_t, slab_near, give = begin(core, slab, sketch_matrix)
    shape = give.shape
    got = lax.ppermute(give, "rows", PAIRS)
    keep = keep_half(core, sketch_t, slab_near)
    mine = all_reduce((keep + got).reshape(-1, 8, 128)).reshape(shape)
    other = lax.ppermute(mine, "rows", PAIRS)
    stack, folded = fold_mine(core, mine, sketch_matrix)
    return finish(core, stack, folded, other, sketch_matrix, sketch_t, math.sqrt(slab.shape[0] * devices))


def solution(mesh):
    return jax.shard_map(
        shards,
        mesh=mesh,
        in_specs=(P("rows", None), P()),
        out_specs=(P(None, "rows"), P(), P(), P()),
        check_vma=False,
    )
```

```python
import functools
import math

import jax
import jax.numpy as jnp
from jax import lax
from jax.experimental import pallas as pl
from jax.experimental.pallas import tpu as pltpu
from jax.sharding import PartitionSpec as P

SIZES = dict(z=8, y=8, x=4, c=2)


def place(index):
    coords = {}
    for name in reversed(SIZES):
        index, coords[name] = divmod(index, SIZES[name])
    return coords


def groups(axes_of_core):
    out = {}
    for index in range(math.prod(SIZES.values())):
        coords = place(index)
        axes = axes_of_core[coords["c"]]
        key = (coords["c"],) + tuple(value for name, value in coords.items() if name not in axes)
        out.setdefault(key, []).append(index)
    return list(out.values())


PLANE = groups(("yx", "zx"))
LINE = groups(("z", "y"))
PAIRS = [(i, i ^ 1) for i in range(math.prod(SIZES.values()))]


def exchange(pieces, peers):
    return lax.all_to_all(pieces, "rows", 0, 0, axis_index_groups=peers, tiled=True)


def summed(tiles, count):
    return tiles.reshape(count, tiles.shape[0] // count, 8, 128).sum(0)


def spread(tiles, peers):
    return exchange(jnp.tile(tiles, (len(peers[0]), 1, 1)), peers)


def all_reduce(part):
    part = summed(exchange(part, PLANE), len(PLANE[0]))
    part = summed(spread(part, LINE), len(LINE[0]))
    return spread(part, PLANE)


LAST = (((1,), (1,)), ((), ()))


def split(value, parts):
    out = []
    for _ in range(parts):
        out.append(value.astype(jnp.bfloat16))
        value = value - out[-1].astype(jnp.float32)
    return out


def eliminate(work, base):
    sub = lax.broadcasted_iota(jnp.int32, (8, 128), 0)

    def row(tile, k):
        return jnp.broadcast_to(tile[k : k + 1, :], (8, 128))

    work = [work[8 * b : 8 * b + 8] for b in range(work.shape[0] // 8)]
    for top in range(len(work)):
        below = range(top + 1, len(work))
        at = base + 8 * top
        column = [
            {b: jnp.broadcast_to(work[b][:, at + k : at + k + 1], (8, 128)) for b in range(top, len(work))}
            for k in range(8)
        ]
        pivot = [row(work[top], k) for k in range(8)]
        m = {(i, k): row(column[k][top], i) for k in range(8) for i in range(k, 8)}
        scaled = []
        for k in range(8):
            inverse = 1.0 / m[k, k]
            scaled.append(pivot[k] * inverse)
            x = {i: m[i, k] * inverse for i in range(k + 1, 8)}
            for i in x:
                for j in range(k + 1, i + 1):
                    m[i, j] = m[i, j] - x[i] * m[j, k]
                pivot[i] = pivot[i] - x[i] * pivot[k]
                for b in below:
                    column[i][b] = column[i][b] - x[i] * column[k][b]
        for b in below:
            terms = [column[k][b] * scaled[k] for k in range(8)]
            while len(terms) > 1:
                terms = [terms[i] + terms[i + 1] for i in range(0, len(terms), 2)]
            work[b] = work[b] - terms[0]
        done = pivot[0]
        for k in range(1, 8):
            done = jnp.where(sub == k, pivot[k], done)
        work[top] = done
    return jnp.concatenate(work, 0)


def factor(gram):
    n = gram.shape[0]
    row = lax.broadcasted_iota(jnp.int32, (n, n), 0)
    col = lax.broadcasted_iota(jnp.int32, (n, n), 1)
    on_diag = jnp.where(row == col, gram, 0.0)
    diag_row = jnp.sum(on_diag, 0, keepdims=True)
    down = lax.rsqrt(jnp.sum(on_diag, 1, keepdims=True))
    across = lax.rsqrt(diag_row)
    scale = jnp.where(row == col, jnp.broadcast_to(down, (n, n)), 0.0)
    work = jnp.concatenate([gram * down * across, scale], 1)
    work = eliminate(work, 0)
    upper = work[:, :n]
    left = lax.rsqrt(jnp.sum(jnp.where(row == col, upper, 0.0), 1, keepdims=True))
    return jnp.where(col >= row, upper * left * (diag_row * across), 0.0), work[:, n:] * left


def pre(widths, core_ref, slab_hbm, sketch_hbm, sketch_t_ref, slab_ref, give_ref, sketch_ref, arrived):
    views, at = [], 0
    for width in widths:
        views.append(pl.ds(at, width))
        at += width
    copies = [
        [
            pltpu.make_async_copy(source.at[:, view], target.at[:, view], arrived.at[j, i])
            for j, (source, target) in enumerate(((sketch_hbm, sketch_ref), (slab_hbm, slab_ref)))
        ]
        for i, view in enumerate(views)
    ]
    for pair in copies:
        for copy in pair:
            copy.start()
    sketch_t = jnp.zeros(sketch_t_ref.shape, jnp.float32)
    for pair, view in zip(copies, views):
        for copy in pair:
            copy.wait()
        sketch_t += lax.dot_general(
            sketch_ref[:, view], slab_ref[:, view], LAST, preferred_element_type=jnp.float32
        )
    sketch_t_ref[...] = sketch_t
    cross_half(1 - core_ref[0], sketch_t, slab_ref, give_ref)


def cross_half(which, sketch_t, slab_ref, out_ref):
    half = slab_ref.shape[1] // 2
    view = pl.ds(pl.multiple_of(which * half, half), half)
    part = jnp.dot(sketch_t.astype(jnp.bfloat16), slab_ref[:, view], preferred_element_type=jnp.float32)
    for b in range(half // 128):
        out_ref[b] = part[:, b * 128 : (b + 1) * 128]


def pre_keep(core_ref, sketch_t_ref, slab_ref, keep_ref):
    cross_half(core_ref[0], sketch_t_ref[...], slab_ref, keep_ref)


SCALAR = pl.BlockSpec(memory_space=pltpu.SMEM)
VMEM = pl.BlockSpec(memory_space=pltpu.VMEM)
LIMIT = pltpu.CompilerParams(vmem_limit_bytes=16 << 20)


def begin(core, slab, sketch_matrix):
    rows, columns = slab.shape
    widths = [columns * part // 16 for part in (1, 3, 5, 7)]
    rank = sketch_matrix.shape[0]
    slab, sketch_matrix = (pltpu.with_memory_space_constraint(a, pltpu.HBM) for a in (slab, sketch_matrix))
    hbm = pl.BlockSpec(memory_space=pltpu.HBM)
    return pl.pallas_call(
        functools.partial(pre, widths),
        out_shape=(
            pltpu.VMEM((rank, rows), jnp.float32),
            pltpu.VMEM(slab.shape, slab.dtype),
            pltpu.VMEM((columns // 256, rank, 128), jnp.float32),
        ),
        in_specs=[SCALAR, hbm, hbm],
        out_specs=[VMEM] * 3,
        scratch_shapes=[
            pltpu.VMEM(sketch_matrix.shape, sketch_matrix.dtype),
            pltpu.SemaphoreType.DMA((2, len(widths))),
        ],
        compiler_params=LIMIT,
        name="sketch_and_cross_to_give",
    )(core, slab, sketch_matrix)


def keep_half(core, sketch_t, slab):
    rows, columns = slab.shape
    rank = sketch_t.shape[0]
    return pl.pallas_call(
        pre_keep,
        out_shape=pltpu.VMEM((columns // 256, rank, 128), jnp.float32),
        in_specs=[SCALAR, VMEM, VMEM],
        out_specs=VMEM,
        compiler_params=LIMIT,
        cost_estimate=pl.CostEstimate(flops=rank * rows * columns, bytes_accessed=slab.size, transcendentals=0),
        name="cross_to_keep",
    )(core, sketch_t, slab)


def right_parts(value):
    high, mid, low = split(value, 3)
    return jnp.concatenate([high, mid, low, high], 0)


def left_parts(value):
    high, mid, low = split(value, 3)
    zero = jnp.zeros_like(high)
    rows = ((high, high, high, low), (mid, mid, zero, zero))
    return jnp.concatenate([jnp.concatenate(parts, 1) for parts in rows], 0)


def fold_half(which, source, sketch_ref, stack):
    rank = sketch_ref.shape[0]
    half = source.shape[0] * 128
    cross = jnp.concatenate([source[b] for b in range(source.shape[0])], 1)
    stack[...] = right_parts(cross)
    view = pl.ds(pl.multiple_of(which * half, half), half)
    out = lax.dot_general(stack[: 3 * rank], sketch_ref[:, view], LAST, preferred_element_type=jnp.float32)
    return out[:rank] + (out[rank : 2 * rank] + out[2 * rank :])


def post_mine(core_ref, mine_ref, sketch_ref, stack, folded_ref):
    folded_ref[...] = fold_half(core_ref[0], mine_ref, sketch_ref, stack)


def fold_mine(core, mine, sketch_matrix):
    rank, columns = sketch_matrix.shape
    return pl.pallas_call(
        post_mine,
        out_shape=(
            pltpu.VMEM((4 * rank, columns // 2), jnp.bfloat16),
            pltpu.VMEM((rank, rank), jnp.float32),
        ),
        in_specs=[SCALAR, VMEM, VMEM],
        out_specs=[VMEM] * 2,
        compiler_params=LIMIT,
        cost_estimate=pl.CostEstimate(
            flops=3 * rank * rank * columns, bytes_accessed=4 * rank * columns, transcendentals=0
        ),
        name="fold_mine",
    )(core, mine, sketch_matrix)


def post(
    root, core_ref, mine_stack, folded_ref, other_ref, sketch_ref, sketch_t_ref, q_ref, proj_ref, tri_ref, gram_ref, other_stack
):
    rank, columns = proj_ref.shape
    half = columns // 2
    core = core_ref[0]
    folded = folded_ref[...] + fold_half(1 - core, other_ref, sketch_ref, other_stack)
    upper, inverse = factor(0.5 * (folded + folded.T))
    tri_ref[...] = upper * (1.0 / root)
    left = left_parts(inverse)
    total = jnp.zeros((2 * rank, rank), jnp.float32)
    for which, stack in ((core, mine_stack), (1 - core, other_stack)):
        for at in range(0, half, 512):
            part = jnp.dot(left, stack[:, at : at + 512], preferred_element_type=jnp.float32)
            part = part[:rank] + part[rank:]
            proj_ref[:, pl.ds(pl.multiple_of(which * half + at, 128), 512)] = part
            pair = split(part, 2)
            total += lax.dot_general(
                jnp.concatenate(pair, 0), pair[0], LAST, preferred_element_type=jnp.float32
            )
    gram_ref[...] = (total[:rank] + (total[rank:] + total[rank:].T)) * (1.0 / columns)
    part = jnp.dot(left_parts(inverse * root), right_parts(sketch_t_ref[...]), preferred_element_type=jnp.float32)
    q_ref[...] = (part[:rank] + part[rank:]).astype(q_ref.dtype)


def finish(core, mine_stack, folded, other, sketch_matrix, sketch_t, root):
    rank, columns = sketch_matrix.shape
    return pl.pallas_call(
        functools.partial(post, root),
        out_shape=(
            jax.ShapeDtypeStruct(sketch_t.shape, jnp.bfloat16),
            jax.ShapeDtypeStruct((rank, columns), jnp.float32),
            jax.ShapeDtypeStruct((rank, rank), jnp.float32),
            jax.ShapeDtypeStruct((rank, rank), jnp.float32),
        ),
        in_specs=[SCALAR] + [VMEM] * 5,
        out_specs=[VMEM] * 4,
        scratch_shapes=[pltpu.VMEM((4 * rank, columns // 2), jnp.bfloat16)],
        compiler_params=pltpu.CompilerParams(vmem_limit_bytes=24 << 20),
        name="factor_and_project",
    )(core, mine_stack, folded, other, sketch_matrix, sketch_t)


def shards(slab, sketch_matrix):
    devices = lax.axis_size("rows")
    core = (lax.axis_index("rows") % 2).reshape(1)
    sketch_t, slab_near, give = begin(core, slab, sketch_matrix)
    shape = give.shape
    got = lax.ppermute(give, "rows", PAIRS)
    keep = keep_half(core, sketch_t, slab_near)
    mine = all_reduce((keep + got).reshape(-1, 8, 128)).reshape(shape)
    other = lax.ppermute(mine, "rows", PAIRS)
    stack, folded = fold_mine(core, mine, sketch_matrix)
    return finish(core, stack, folded, other, sketch_matrix, sketch_t, math.sqrt(slab.shape[0] * devices))


def solution(mesh):
    return jax.shard_map(
        shards,
        mesh=mesh,
        in_specs=(P("rows", None), P()),
        out_specs=(P(None, "rows"), P(), P(), P()),
        check_vma=False,
    )
```

```python
import functools
import math

import jax
import jax.numpy as jnp
from jax import lax
from jax.experimental import pallas as pl
from jax.experimental.pallas import tpu as pltpu
from jax.sharding import PartitionSpec as P

SIZES = dict(z=8, y=8, x=4, c=2)


def place(index):
    coords = {}
    for name in reversed(SIZES):
        index, coords[name] = divmod(index, SIZES[name])
    return coords


def groups(axes_of_core):
    out = {}
    for index in range(math.prod(SIZES.values())):
        coords = place(index)
        axes = axes_of_core[coords["c"]]
        key = (coords["c"],) + tuple(value for name, value in coords.items() if name not in axes)
        out.setdefault(key, []).append(index)
    return list(out.values())


PLANE = groups(("zx", "yx"))
LINE = groups(("y", "z"))
PAIRS = [(i, i ^ 1) for i in range(math.prod(SIZES.values()))]


def exchange(pieces, peers):
    return lax.all_to_all(pieces, "rows", 0, 0, axis_index_groups=peers, tiled=True)


def summed(tiles, count):
    return tiles.reshape(count, tiles.shape[0] // count, 8, 128).sum(0)


def spread(tiles, peers):
    return exchange(jnp.tile(tiles, (len(peers[0]), 1, 1)), peers)


def all_reduce(part):
    part = summed(exchange(part, PLANE), len(PLANE[0]))
    part = summed(spread(part, LINE), len(LINE[0]))
    return spread(part, PLANE)


LAST = (((1,), (1,)), ((), ()))


def split(value, parts):
    out = []
    for _ in range(parts):
        out.append(value.astype(jnp.bfloat16))
        value = value - out[-1].astype(jnp.float32)
    return out


def eliminate(work, base):
    sub = lax.broadcasted_iota(jnp.int32, (8, 128), 0)

    def row(tile, k):
        return jnp.broadcast_to(tile[k : k + 1, :], (8, 128))

    work = [work[8 * b : 8 * b + 8] for b in range(work.shape[0] // 8)]
    for top in range(len(work)):
        below = range(top + 1, len(work))
        at = base + 8 * top
        column = [
            {b: jnp.broadcast_to(work[b][:, at + k : at + k + 1], (8, 128)) for b in range(top, len(work))}
            for k in range(8)
        ]
        pivot = [row(work[top], k) for k in range(8)]
        m = {(i, k): row(column[k][top], i) for k in range(8) for i in range(k, 8)}
        scaled = []
        for k in range(8):
            inverse = 1.0 / m[k, k]
            scaled.append(pivot[k] * inverse)
            x = {i: m[i, k] * inverse for i in range(k + 1, 8)}
            for i in x:
                for j in range(k + 1, i + 1):
                    m[i, j] = m[i, j] - x[i] * m[j, k]
                pivot[i] = pivot[i] - x[i] * pivot[k]
                for b in below:
                    column[i][b] = column[i][b] - x[i] * column[k][b]
        for b in below:
            terms = [column[k][b] * scaled[k] for k in range(8)]
            while len(terms) > 1:
                terms = [terms[i] + terms[i + 1] for i in range(0, len(terms), 2)]
            work[b] = work[b] - terms[0]
        done = pivot[0]
        for k in range(1, 8):
            done = jnp.where(sub == k, pivot[k], done)
        work[top] = done
    return jnp.concatenate(work, 0)


def factor(gram):
    n = gram.shape[0]
    row = lax.broadcasted_iota(jnp.int32, (n, n), 0)
    col = lax.broadcasted_iota(jnp.int32, (n, n), 1)
    on_diag = jnp.where(row == col, gram, 0.0)
    diag_row = jnp.sum(on_diag, 0, keepdims=True)
    down = lax.rsqrt(jnp.sum(on_diag, 1, keepdims=True))
    across = lax.rsqrt(diag_row)
    scale = jnp.where(row == col, jnp.broadcast_to(down, (n, n)), 0.0)
    work = jnp.concatenate([gram * down * across, scale], 1)
    work = eliminate(work, 0)
    upper = work[:, :n]
    left = lax.rsqrt(jnp.sum(jnp.where(row == col, upper, 0.0), 1, keepdims=True))
    return jnp.where(col >= row, upper * left * (diag_row * across), 0.0), work[:, n:] * left


def pre(widths, core_ref, slab_hbm, sketch_hbm, sketch_t_ref, slab_ref, give_ref, sketch_ref, arrived):
    views, at = [], 0
    for width in widths:
        views.append(pl.ds(at, width))
        at += width
    copies = [
        [
            pltpu.make_async_copy(source.at[:, view], target.at[:, view], arrived.at[j, i])
            for j, (source, target) in enumerate(((sketch_hbm, sketch_ref), (slab_hbm, slab_ref)))
        ]
        for i, view in enumerate(views)
    ]
    for pair in copies:
        for copy in pair:
            copy.start()
    sketch_t = jnp.zeros(sketch_t_ref.shape, jnp.float32)
    for pair, view in zip(copies, views):
        for copy in pair:
            copy.wait()
        sketch_t += lax.dot_general(
            sketch_ref[:, view], slab_ref[:, view], LAST, preferred_element_type=jnp.float32
        )
    sketch_t_ref[...] = sketch_t
    cross_half(1 - core_ref[0], sketch_t, slab_ref, give_ref)


def cross_half(which, sketch_t, slab_ref, out_ref):
    half = slab_ref.shape[1] // 2
    view = pl.ds(pl.multiple_of(which * half, half), half)
    part = jnp.dot(sketch_t.astype(jnp.bfloat16), slab_ref[:, view], preferred_element_type=jnp.float32)
    for b in range(half // 128):
        out_ref[b] = part[:, b * 128 : (b + 1) * 128]


def pre_keep(core_ref, sketch_t_ref, slab_ref, keep_ref):
    cross_half(core_ref[0], sketch_t_ref[...], slab_ref, keep_ref)


SCALAR = pl.BlockSpec(memory_space=pltpu.SMEM)
VMEM = pl.BlockSpec(memory_space=pltpu.VMEM)
LIMIT = pltpu.CompilerParams(vmem_limit_bytes=16 << 20)


def begin(core, slab, sketch_matrix):
    rows, columns = slab.shape
    widths = [columns * part // 16 for part in (1, 3, 5, 7)]
    rank = sketch_matrix.shape[0]
    slab, sketch_matrix = (pltpu.with_memory_space_constraint(a, pltpu.HBM) for a in (slab, sketch_matrix))
    hbm = pl.BlockSpec(memory_space=pltpu.HBM)
    return pl.pallas_call(
        functools.partial(pre, widths),
        out_shape=(
            pltpu.VMEM((rank, rows), jnp.float32),
            pltpu.VMEM(slab.shape, slab.dtype),
            pltpu.VMEM((columns // 256, rank, 128), jnp.float32),
        ),
        in_specs=[SCALAR, hbm, hbm],
        out_specs=[VMEM] * 3,
        scratch_shapes=[
            pltpu.VMEM(sketch_matrix.shape, sketch_matrix.dtype),
            pltpu.SemaphoreType.DMA((2, len(widths))),
        ],
        compiler_params=LIMIT,
        name="sketch_and_cross_to_give",
    )(core, slab, sketch_matrix)


def keep_half(core, sketch_t, slab):
    rows, columns = slab.shape
    rank = sketch_t.shape[0]
    return pl.pallas_call(
        pre_keep,
        out_shape=pltpu.VMEM((columns // 256, rank, 128), jnp.float32),
        in_specs=[SCALAR, VMEM, VMEM],
        out_specs=VMEM,
        compiler_params=LIMIT,
        cost_estimate=pl.CostEstimate(flops=rank * rows * columns, bytes_accessed=slab.size, transcendentals=0),
        name="cross_to_keep",
    )(core, sketch_t, slab)


def right_parts(value):
    high, mid, low = split(value, 3)
    return jnp.concatenate([high, mid, low, high], 0)


def left_parts(value):
    high, mid, low = split(value, 3)
    zero = jnp.zeros_like(high)
    rows = ((high, high, high, low), (mid, mid, zero, zero))
    return jnp.concatenate([jnp.concatenate(parts, 1) for parts in rows], 0)


def fold_half(which, source, sketch_ref, stack):
    rank = sketch_ref.shape[0]
    half = source.shape[0] * 128
    cross = jnp.concatenate([source[b] for b in range(source.shape[0])], 1)
    stack[...] = right_parts(cross)
    view = pl.ds(pl.multiple_of(which * half, half), half)
    out = lax.dot_general(stack[: 3 * rank], sketch_ref[:, view], LAST, preferred_element_type=jnp.float32)
    return out[:rank] + (out[rank : 2 * rank] + out[2 * rank :])


def post_mine(core_ref, mine_ref, sketch_ref, stack, folded_ref):
    folded_ref[...] = fold_half(core_ref[0], mine_ref, sketch_ref, stack)


def fold_mine(core, mine, sketch_matrix):
    rank, columns = sketch_matrix.shape
    return pl.pallas_call(
        post_mine,
        out_shape=(
            pltpu.VMEM((4 * rank, columns // 2), jnp.bfloat16),
            pltpu.VMEM((rank, rank), jnp.float32),
        ),
        in_specs=[SCALAR, VMEM, VMEM],
        out_specs=[VMEM] * 2,
        compiler_params=LIMIT,
        cost_estimate=pl.CostEstimate(
            flops=3 * rank * rank * columns, bytes_accessed=4 * rank * columns, transcendentals=0
        ),
        name="fold_mine",
    )(core, mine, sketch_matrix)


def post(
    root, core_ref, mine_stack, folded_ref, other_ref, sketch_ref, sketch_t_ref, q_ref, proj_ref, tri_ref, gram_ref, other_stack
):
    rank, columns = proj_ref.shape
    half = columns // 2
    core = core_ref[0]
    folded = folded_ref[...] + fold_half(1 - core, other_ref, sketch_ref, other_stack)
    upper, inverse = factor(0.5 * (folded + folded.T))
    tri_ref[...] = upper * (1.0 / root)
    left = left_parts(inverse)
    total = jnp.zeros((2 * rank, rank), jnp.float32)
    for which, stack in ((core, mine_stack), (1 - core, other_stack)):
        for at in range(0, half, 512):
            part = jnp.dot(left, stack[:, at : at + 512], preferred_element_type=jnp.float32)
            part = part[:rank] + part[rank:]
            proj_ref[:, pl.ds(pl.multiple_of(which * half + at, 128), 512)] = part
            pair = split(part, 2)
            total += lax.dot_general(
                jnp.concatenate(pair, 0), pair[0], LAST, preferred_element_type=jnp.float32
            )
    gram_ref[...] = (total[:rank] + (total[rank:] + total[rank:].T)) * (1.0 / columns)
    part = jnp.dot(left_parts(inverse * root), right_parts(sketch_t_ref[...]), preferred_element_type=jnp.float32)
    q_ref[...] = (part[:rank] + part[rank:]).astype(q_ref.dtype)


def finish(core, mine_stack, folded, other, sketch_matrix, sketch_t, root):
    rank, columns = sketch_matrix.shape
    return pl.pallas_call(
        functools.partial(post, root),
        out_shape=(
            jax.ShapeDtypeStruct(sketch_t.shape, jnp.bfloat16),
            jax.ShapeDtypeStruct((rank, columns), jnp.float32),
            jax.ShapeDtypeStruct((rank, rank), jnp.float32),
            jax.ShapeDtypeStruct((rank, rank), jnp.float32),
        ),
        in_specs=[SCALAR] + [VMEM] * 5,
        out_specs=[VMEM] * 4,
        scratch_shapes=[pltpu.VMEM((4 * rank, columns // 2), jnp.bfloat16)],
        compiler_params=pltpu.CompilerParams(vmem_limit_bytes=24 << 20),
        name="factor_and_project",
    )(core, mine_stack, folded, other, sketch_matrix, sketch_t)


def shards(slab, sketch_matrix):
    devices = lax.axis_size("rows")
    core = (lax.axis_index("rows") % 2).reshape(1)
    sketch_t, slab_near, give = begin(core, slab, sketch_matrix)
    shape = give.shape
    got = lax.ppermute(give, "rows", PAIRS)
    keep = keep_half(core, sketch_t, slab_near)
    mine = all_reduce((keep + got).reshape(-1, 8, 128)).reshape(shape)
    other = lax.ppermute(mine, "rows", PAIRS)
    stack, folded = fold_mine(core, mine, sketch_matrix)
    return finish(core, stack, folded, other, sketch_matrix, sketch_t, math.sqrt(slab.shape[0] * devices))


def solution(mesh):
    return jax.shard_map(
        shards,
        mesh=mesh,
        in_specs=(P("rows", None), P()),
        out_specs=(P(None, "rows"), P(), P(), P()),
        check_vma=False,
    )
```

```python
import functools
import math

import jax
import jax.numpy as jnp
from jax import lax
from jax.experimental import pallas as pl
from jax.experimental.pallas import tpu as pltpu
from jax.sharding import PartitionSpec as P

SIZES = dict(z=8, y=8, x=4, c=2)


def place(index):
    coords = {}
    for name in reversed(SIZES):
        index, coords[name] = divmod(index, SIZES[name])
    return coords


def groups(axes_of_core):
    out = {}
    for index in range(math.prod(SIZES.values())):
        coords = place(index)
        axes = axes_of_core[coords["c"]]
        key = (coords["c"],) + tuple(value for name, value in coords.items() if name not in axes)
        out.setdefault(key, []).append(index)
    return list(out.values())


PLANE = groups(("yx", "zx"))
LINE = groups(("z", "y"))
PAIRS = [(i, i ^ 1) for i in range(math.prod(SIZES.values()))]


def exchange(pieces, peers):
    return lax.all_to_all(pieces, "rows", 0, 0, axis_index_groups=peers, tiled=True)


def total_kernel(size, got_ref, out_ref):
    senders, receivers = got_ref.shape[0] // size, out_ref.shape[0] // size
    for t in range(size):
        terms = [got_ref[k * size + t] for k in range(senders)]
        while len(terms) > 1:
            terms = [terms[i] + terms[i + 1] for i in range(0, len(terms), 2)]
        for k in range(receivers):
            out_ref[k * size + t] = terms[0]


def total(got, size, receivers):
    vmem = pl.BlockSpec(memory_space=pltpu.VMEM)
    return pl.pallas_call(
        functools.partial(total_kernel, size),
        out_shape=pltpu.VMEM((size * receivers, 8, 128), jnp.float32),
        in_specs=[vmem],
        out_specs=vmem,
        compiler_params=pltpu.CompilerParams(vmem_limit_bytes=16 << 20),
        name="sum_and_repeat",
    )(got)


def all_reduce(part):
    plane, line = len(PLANE[0]), len(LINE[0])
    size = part.shape[0] // plane
    got = exchange(total(exchange(part, PLANE), size, line), LINE)
    return exchange(total(got, size, plane), PLANE)


LAST = (((1,), (1,)), ((), ()))


def split(value, parts):
    out = []
    for _ in range(parts):
        out.append(value.astype(jnp.bfloat16))
        value = value - out[-1].astype(jnp.float32)
    return out


def eliminate(work, base, size=16):
    sub = lax.broadcasted_iota(jnp.int32, (8, 128), 0)

    def row(tile, k):
        return jnp.broadcast_to(tile[k : k + 1, :], (8, 128))

    work = [work[8 * b : 8 * b + 8] for b in range(work.shape[0] // 8)]
    for first in range(0, 8 * len(work), size):
        top, off = divmod(first, 8)
        tops = range(top, (first + size + 7) // 8)
        ends_inside = (first + size) % 8 != 0
        below = range(tops[-1] if ends_inside else tops[-1] + 1, len(work))
        at = base + first
        column = [
            {b: jnp.broadcast_to(work[b][:, at + k : at + k + 1], (8, 128)) for b in range(top, len(work))}
            for k in range(size)
        ]
        pivot = [row(work[(first + k) // 8], (first + k) % 8) for k in range(size)]
        m = {(i, k): row(column[k][(first + i) // 8], (first + i) % 8) for k in range(size) for i in range(k, size)}
        scaled = []
        for k in range(size):
            inverse = 1.0 / m[k, k]
            scaled.append(pivot[k] * inverse)
            x = {i: m[i, k] * inverse for i in range(k + 1, size)}
            for i in x:
                for j in range(k + 1, i + 1):
                    m[i, j] = m[i, j] - x[i] * m[j, k]
                pivot[i] = pivot[i] - x[i] * pivot[k]
                for b in below:
                    column[i][b] = column[i][b] - x[i] * column[k][b]
        new = {}
        for b in below:
            terms = [column[k][b] * scaled[k] for k in range(size)]
            while len(terms) > 1:
                terms = [terms[i] + terms[i + 1] for i in range(0, len(terms), 2)]
            new[b] = work[b] - terms[0]
        for b in tops:
            done = new.get(b, work[b])
            if ends_inside or off:
                done = jnp.where(sub >= off + size, done, work[b])
            for k in range(size):
                if (first + k) // 8 == b:
                    done = jnp.where(sub == (first + k) % 8, pivot[k], done)
            new[b] = done
        for b in new:
            work[b] = new[b]
    return jnp.concatenate(work, 0)


def factor(gram):
    n = gram.shape[0]
    row = lax.broadcasted_iota(jnp.int32, (n, n), 0)
    col = lax.broadcasted_iota(jnp.int32, (n, n), 1)
    on_diag = jnp.where(row == col, gram, 0.0)
    diag_row = jnp.sum(on_diag, 0, keepdims=True)
    down = lax.rsqrt(jnp.sum(on_diag, 1, keepdims=True))
    across = lax.rsqrt(diag_row)
    scale = jnp.where(row == col, jnp.broadcast_to(down, (n, n)), 0.0)
    work = jnp.concatenate([gram * down * across, scale], 1)
    work = eliminate(work, 0)
    upper = work[:, :n]
    left = lax.rsqrt(jnp.sum(jnp.where(row == col, upper, 0.0), 1, keepdims=True))
    return jnp.where(col >= row, upper * left * (diag_row * across), 0.0), work[:, n:] * left


def pre(widths, core_ref, slab_hbm, sketch_hbm, sketch_t_ref, slab_ref, give_ref, sketch_ref, arrived):
    views, at = [], 0
    for width in widths:
        views.append(pl.ds(at, width))
        at += width
    copies = [
        [
            pltpu.make_async_copy(source.at[:, view], target.at[:, view], arrived.at[j, i])
            for j, (source, target) in enumerate(((sketch_hbm, sketch_ref), (slab_hbm, slab_ref)))
        ]
        for i, view in enumerate(views)
    ]
    for pair in copies:
        for copy in pair:
            copy.start()
    sketch_t = jnp.zeros(sketch_t_ref.shape, jnp.float32)
    for pair, view in zip(copies, views):
        for copy in pair:
            copy.wait()
        sketch_t += lax.dot_general(
            sketch_ref[:, view], slab_ref[:, view], LAST, preferred_element_type=jnp.float32
        )
    sketch_t_ref[...] = sketch_t
    cross_half(1 - core_ref[0], sketch_t, slab_ref, give_ref)


def cross_half(which, sketch_t, slab_ref, out_ref):
    half = slab_ref.shape[1] // 2
    view = pl.ds(pl.multiple_of(which * half, half), half)
    part = jnp.dot(sketch_t.astype(jnp.bfloat16), slab_ref[:, view], preferred_element_type=jnp.float32)
    for b in range(half // 128):
        out_ref[b] = part[:, b * 128 : (b + 1) * 128]


def pre_keep(core_ref, sketch_t_ref, slab_ref, keep_ref):
    cross_half(core_ref[0], sketch_t_ref[...], slab_ref, keep_ref)


SCALAR = pl.BlockSpec(memory_space=pltpu.SMEM)
VMEM = pl.BlockSpec(memory_space=pltpu.VMEM)
LIMIT = pltpu.CompilerParams(vmem_limit_bytes=16 << 20)


def begin(core, slab, sketch_matrix):
    rows, columns = slab.shape
    widths = [columns * part // 16 for part in (1, 3, 5, 7)]
    rank = sketch_matrix.shape[0]
    slab, sketch_matrix = (pltpu.with_memory_space_constraint(a, pltpu.HBM) for a in (slab, sketch_matrix))
    hbm = pl.BlockSpec(memory_space=pltpu.HBM)
    return pl.pallas_call(
        functools.partial(pre, widths),
        out_shape=(
            pltpu.VMEM((rank, rows), jnp.float32),
            pltpu.VMEM(slab.shape, slab.dtype),
            pltpu.VMEM((columns // 256, rank, 128), jnp.float32),
        ),
        in_specs=[SCALAR, hbm, hbm],
        out_specs=[VMEM] * 3,
        scratch_shapes=[
            pltpu.VMEM(sketch_matrix.shape, sketch_matrix.dtype),
            pltpu.SemaphoreType.DMA((2, len(widths))),
        ],
        compiler_params=LIMIT,
        name="sketch_and_cross_to_give",
    )(core, slab, sketch_matrix)


def keep_half(core, sketch_t, slab):
    rows, columns = slab.shape
    rank = sketch_t.shape[0]
    return pl.pallas_call(
        pre_keep,
        out_shape=pltpu.VMEM((columns // 256, rank, 128), jnp.float32),
        in_specs=[SCALAR, VMEM, VMEM],
        out_specs=VMEM,
        compiler_params=LIMIT,
        cost_estimate=pl.CostEstimate(flops=rank * rows * columns, bytes_accessed=slab.size, transcendentals=0),
        name="cross_to_keep",
    )(core, sketch_t, slab)


def right_parts(value):
    high, mid, low = split(value, 3)
    return jnp.concatenate([high, mid, low, high], 0)


def left_parts(value):
    high, mid, low = split(value, 3)
    zero = jnp.zeros_like(high)
    rows = ((high, high, high, low), (mid, mid, zero, zero))
    return jnp.concatenate([jnp.concatenate(parts, 1) for parts in rows], 0)


def fold_half(which, source, sketch_ref, stack):
    rank = sketch_ref.shape[0]
    half = source.shape[0] * 128
    cross = jnp.concatenate([source[b] for b in range(source.shape[0])], 1)
    stack[...] = right_parts(cross)
    view = pl.ds(pl.multiple_of(which * half, half), half)
    out = lax.dot_general(stack[: 3 * rank], sketch_ref[:, view], LAST, preferred_element_type=jnp.float32)
    return out[:rank] + (out[rank : 2 * rank] + out[2 * rank :])


def post_mine(core_ref, mine_ref, sketch_ref, stack, folded_ref):
    folded_ref[...] = fold_half(core_ref[0], mine_ref, sketch_ref, stack)


def fold_mine(core, mine, sketch_matrix):
    rank, columns = sketch_matrix.shape
    return pl.pallas_call(
        post_mine,
        out_shape=(
            pltpu.VMEM((4 * rank, columns // 2), jnp.bfloat16),
            pltpu.VMEM((rank, rank), jnp.float32),
        ),
        in_specs=[SCALAR, VMEM, VMEM],
        out_specs=[VMEM] * 2,
        compiler_params=LIMIT,
        cost_estimate=pl.CostEstimate(
            flops=3 * rank * rank * columns, bytes_accessed=4 * rank * columns, transcendentals=0
        ),
        name="fold_mine",
    )(core, mine, sketch_matrix)


def post(
    root, core_ref, mine_stack, folded_ref, other_ref, sketch_ref, sketch_t_ref, q_ref, proj_ref, tri_ref, gram_ref, other_stack
):
    rank, columns = proj_ref.shape
    half = columns // 2
    core = core_ref[0]
    folded = folded_ref[...] + fold_half(1 - core, other_ref, sketch_ref, other_stack)
    upper, inverse = factor(0.5 * (folded + folded.T))
    tri_ref[...] = upper * (1.0 / root)
    left = left_parts(inverse)
    total = jnp.zeros((2 * rank, rank), jnp.float32)
    for which, stack in ((core, mine_stack), (1 - core, other_stack)):
        for at in range(0, half, 512):
            part = jnp.dot(left, stack[:, at : at + 512], preferred_element_type=jnp.float32)
            part = part[:rank] + part[rank:]
            proj_ref[:, pl.ds(pl.multiple_of(which * half + at, 128), 512)] = part
            pair = split(part, 2)
            total += lax.dot_general(
                jnp.concatenate(pair, 0), pair[0], LAST, preferred_element_type=jnp.float32
            )
    gram_ref[...] = (total[:rank] + (total[rank:] + total[rank:].T)) * (1.0 / columns)
    part = jnp.dot(left_parts(inverse * root), right_parts(sketch_t_ref[...]), preferred_element_type=jnp.float32)
    q_ref[...] = (part[:rank] + part[rank:]).astype(q_ref.dtype)


def finish(core, mine_stack, folded, other, sketch_matrix, sketch_t, root):
    rank, columns = sketch_matrix.shape
    return pl.pallas_call(
        functools.partial(post, root),
        out_shape=(
            jax.ShapeDtypeStruct(sketch_t.shape, jnp.bfloat16),
            jax.ShapeDtypeStruct((rank, columns), jnp.float32),
            jax.ShapeDtypeStruct((rank, rank), jnp.float32),
            jax.ShapeDtypeStruct((rank, rank), jnp.float32),
        ),
        in_specs=[SCALAR] + [VMEM] * 5,
        out_specs=[VMEM] * 4,
        scratch_shapes=[pltpu.VMEM((4 * rank, columns // 2), jnp.bfloat16)],
        compiler_params=pltpu.CompilerParams(vmem_limit_bytes=24 << 20),
        name="factor_and_project",
    )(core, mine_stack, folded, other, sketch_matrix, sketch_t)


def shards(slab, sketch_matrix):
    devices = lax.axis_size("rows")
    core = (lax.axis_index("rows") % 2).reshape(1)
    sketch_t, slab_near, give = begin(core, slab, sketch_matrix)
    shape = give.shape
    got = lax.ppermute(give, "rows", PAIRS)
    keep = keep_half(core, sketch_t, slab_near)
    mine = all_reduce((keep + got).reshape(-1, 8, 128)).reshape(shape)
    other = lax.ppermute(mine, "rows", PAIRS)
    stack, folded = fold_mine(core, mine, sketch_matrix)
    return finish(core, stack, folded, other, sketch_matrix, sketch_t, math.sqrt(slab.shape[0] * devices))


def solution(mesh):
    return jax.shard_map(
        shards,
        mesh=mesh,
        in_specs=(P("rows", None), P()),
        out_specs=(P(None, "rows"), P(), P(), P()),
        check_vma=False,
    )
```

```python
import functools
import math

import jax
import jax.numpy as jnp
from jax import lax
from jax.experimental import pallas as pl
from jax.experimental.pallas import tpu as pltpu
from jax.sharding import PartitionSpec as P

SIZES = dict(z=8, y=8, x=4, c=2)


def place(index):
    coords = {}
    for name in reversed(SIZES):
        index, coords[name] = divmod(index, SIZES[name])
    return coords


def groups(held):
    out = {}
    for index in range(math.prod(SIZES.values())):
        out.setdefault(held(**place(index)), []).append(index)
    return list(out.values())


NEAR = groups(lambda x, y, z, c: (c, y // 2, z // 2))
FAR = groups(lambda x, y, z, c: (c, x, y % 2, z % 2))
PAIRS = [(i, i ^ 1) for i in range(math.prod(SIZES.values()))]


def exchange(pieces, peers):
    return lax.all_to_all(pieces, "rows", 0, 0, axis_index_groups=peers, tiled=True)


def summed(tiles, count):
    return tiles.reshape(count, tiles.shape[0] // count, 8, 128).sum(0)


def spread(tiles, peers):
    return exchange(jnp.tile(tiles, (len(peers[0]), 1, 1)), peers)


def all_reduce(part):
    part = summed(exchange(part, NEAR), len(NEAR[0]))
    part = summed(spread(part, FAR), len(FAR[0]))
    return spread(part, NEAR)


LAST = (((1,), (1,)), ((), ()))


def split(value, parts):
    out = []
    for _ in range(parts):
        out.append(value.astype(jnp.bfloat16))
        value = value - out[-1].astype(jnp.float32)
    return out


def eliminate(work, base):
    sub = lax.broadcasted_iota(jnp.int32, (8, 128), 0)

    def row(tile, k):
        return jnp.broadcast_to(tile[k : k + 1, :], (8, 128))

    work = [work[8 * b : 8 * b + 8] for b in range(work.shape[0] // 8)]
    for top in range(len(work)):
        below = range(top + 1, len(work))
        at = base + 8 * top
        column = [
            {b: jnp.broadcast_to(work[b][:, at + k : at + k + 1], (8, 128)) for b in range(top, len(work))}
            for k in range(8)
        ]
        pivot = [row(work[top], k) for k in range(8)]
        m = {(i, k): row(column[k][top], i) for k in range(8) for i in range(k, 8)}
        scaled = []
        for k in range(8):
            inverse = 1.0 / m[k, k]
            scaled.append(pivot[k] * inverse)
            x = {i: m[i, k] * inverse for i in range(k + 1, 8)}
            for i in x:
                for j in range(k + 1, i + 1):
                    m[i, j] = m[i, j] - x[i] * m[j, k]
                pivot[i] = pivot[i] - x[i] * pivot[k]
                for b in below:
                    column[i][b] = column[i][b] - x[i] * column[k][b]
        for b in below:
            terms = [column[k][b] * scaled[k] for k in range(8)]
            while len(terms) > 1:
                terms = [terms[i] + terms[i + 1] for i in range(0, len(terms), 2)]
            work[b] = work[b] - terms[0]
        done = pivot[0]
        for k in range(1, 8):
            done = jnp.where(sub == k, pivot[k], done)
        work[top] = done
    return jnp.concatenate(work, 0)


def factor(gram):
    n = gram.shape[0]
    row = lax.broadcasted_iota(jnp.int32, (n, n), 0)
    col = lax.broadcasted_iota(jnp.int32, (n, n), 1)
    on_diag = jnp.where(row == col, gram, 0.0)
    diag_row = jnp.sum(on_diag, 0, keepdims=True)
    down = lax.rsqrt(jnp.sum(on_diag, 1, keepdims=True))
    across = lax.rsqrt(diag_row)
    scale = jnp.where(row == col, jnp.broadcast_to(down, (n, n)), 0.0)
    work = jnp.concatenate([gram * down * across, scale], 1)
    work = eliminate(work, 0)
    upper = work[:, :n]
    left = lax.rsqrt(jnp.sum(jnp.where(row == col, upper, 0.0), 1, keepdims=True))
    return jnp.where(col >= row, upper * left * (diag_row * across), 0.0), work[:, n:] * left


def pre(widths, core_ref, slab_hbm, sketch_hbm, sketch_t_ref, slab_ref, give_ref, sketch_ref, arrived):
    views, at = [], 0
    for width in widths:
        views.append(pl.ds(at, width))
        at += width
    copies = [
        [
            pltpu.make_async_copy(source.at[:, view], target.at[:, view], arrived.at[j, i])
            for j, (source, target) in enumerate(((sketch_hbm, sketch_ref), (slab_hbm, slab_ref)))
        ]
        for i, view in enumerate(views)
    ]
    for pair in copies:
        for copy in pair:
            copy.start()
    sketch_t = jnp.zeros(sketch_t_ref.shape, jnp.float32)
    for pair, view in zip(copies, views):
        for copy in pair:
            copy.wait()
        sketch_t += lax.dot_general(
            sketch_ref[:, view], slab_ref[:, view], LAST, preferred_element_type=jnp.float32
        )
    sketch_t_ref[...] = sketch_t
    cross_half(1 - core_ref[0], sketch_t, slab_ref, give_ref)


def cross_half(which, sketch_t, slab_ref, out_ref):
    half = slab_ref.shape[1] // 2
    view = pl.ds(pl.multiple_of(which * half, half), half)
    part = jnp.dot(sketch_t.astype(jnp.bfloat16), slab_ref[:, view], preferred_element_type=jnp.float32)
    for b in range(half // 128):
        out_ref[b] = part[:, b * 128 : (b + 1) * 128]


def pre_keep(core_ref, sketch_t_ref, slab_ref, keep_ref):
    cross_half(core_ref[0], sketch_t_ref[...], slab_ref, keep_ref)


SCALAR = pl.BlockSpec(memory_space=pltpu.SMEM)
VMEM = pl.BlockSpec(memory_space=pltpu.VMEM)
LIMIT = pltpu.CompilerParams(vmem_limit_bytes=16 << 20)


def begin(core, slab, sketch_matrix):
    rows, columns = slab.shape
    widths = [columns * part // 16 for part in (1, 3, 5, 7)]
    rank = sketch_matrix.shape[0]
    slab, sketch_matrix = (pltpu.with_memory_space_constraint(a, pltpu.HBM) for a in (slab, sketch_matrix))
    hbm = pl.BlockSpec(memory_space=pltpu.HBM)
    return pl.pallas_call(
        functools.partial(pre, widths),
        out_shape=(
            pltpu.VMEM((rank, rows), jnp.float32),
            pltpu.VMEM(slab.shape, slab.dtype),
            pltpu.VMEM((columns // 256, rank, 128), jnp.float32),
        ),
        in_specs=[SCALAR, hbm, hbm],
        out_specs=[VMEM] * 3,
        scratch_shapes=[
            pltpu.VMEM(sketch_matrix.shape, sketch_matrix.dtype),
            pltpu.SemaphoreType.DMA((2, len(widths))),
        ],
        compiler_params=LIMIT,
        name="sketch_and_cross_to_give",
    )(core, slab, sketch_matrix)


def keep_half(core, sketch_t, slab):
    rows, columns = slab.shape
    rank = sketch_t.shape[0]
    return pl.pallas_call(
        pre_keep,
        out_shape=pltpu.VMEM((columns // 256, rank, 128), jnp.float32),
        in_specs=[SCALAR, VMEM, VMEM],
        out_specs=VMEM,
        compiler_params=LIMIT,
        cost_estimate=pl.CostEstimate(flops=rank * rows * columns, bytes_accessed=slab.size, transcendentals=0),
        name="cross_to_keep",
    )(core, sketch_t, slab)


def right_parts(value):
    high, mid, low = split(value, 3)
    return jnp.concatenate([high, mid, low, high], 0)


def left_parts(value):
    high, mid, low = split(value, 3)
    zero = jnp.zeros_like(high)
    rows = ((high, high, high, low), (mid, mid, zero, zero))
    return jnp.concatenate([jnp.concatenate(parts, 1) for parts in rows], 0)


def fold_half(which, source, sketch_ref, stack):
    rank = sketch_ref.shape[0]
    half = source.shape[0] * 128
    cross = jnp.concatenate([source[b] for b in range(source.shape[0])], 1)
    stack[...] = right_parts(cross)
    view = pl.ds(pl.multiple_of(which * half, half), half)
    out = lax.dot_general(stack[: 3 * rank], sketch_ref[:, view], LAST, preferred_element_type=jnp.float32)
    return out[:rank] + (out[rank : 2 * rank] + out[2 * rank :])


def post_mine(core_ref, mine_ref, sketch_ref, stack, folded_ref):
    folded_ref[...] = fold_half(core_ref[0], mine_ref, sketch_ref, stack)


def fold_mine(core, mine, sketch_matrix):
    rank, columns = sketch_matrix.shape
    return pl.pallas_call(
        post_mine,
        out_shape=(
            pltpu.VMEM((4 * rank, columns // 2), jnp.bfloat16),
            pltpu.VMEM((rank, rank), jnp.float32),
        ),
        in_specs=[SCALAR, VMEM, VMEM],
        out_specs=[VMEM] * 2,
        compiler_params=LIMIT,
        cost_estimate=pl.CostEstimate(
            flops=3 * rank * rank * columns, bytes_accessed=4 * rank * columns, transcendentals=0
        ),
        name="fold_mine",
    )(core, mine, sketch_matrix)


def post(
    root, core_ref, mine_stack, folded_ref, other_ref, sketch_ref, sketch_t_ref, q_ref, proj_ref, tri_ref, gram_ref, other_stack
):
    rank, columns = proj_ref.shape
    half = columns // 2
    core = core_ref[0]
    folded = folded_ref[...] + fold_half(1 - core, other_ref, sketch_ref, other_stack)
    upper, inverse = factor(0.5 * (folded + folded.T))
    tri_ref[...] = upper * (1.0 / root)
    left = left_parts(inverse)
    total = jnp.zeros((2 * rank, rank), jnp.float32)
    for which, stack in ((core, mine_stack), (1 - core, other_stack)):
        for at in range(0, half, 512):
            part = jnp.dot(left, stack[:, at : at + 512], preferred_element_type=jnp.float32)
            part = part[:rank] + part[rank:]
            proj_ref[:, pl.ds(pl.multiple_of(which * half + at, 128), 512)] = part
            pair = split(part, 2)
            total += lax.dot_general(
                jnp.concatenate(pair, 0), pair[0], LAST, preferred_element_type=jnp.float32
            )
    gram_ref[...] = (total[:rank] + (total[rank:] + total[rank:].T)) * (1.0 / columns)
    part = jnp.dot(left_parts(inverse * root), right_parts(sketch_t_ref[...]), preferred_element_type=jnp.float32)
    q_ref[...] = (part[:rank] + part[rank:]).astype(q_ref.dtype)


def finish(core, mine_stack, folded, other, sketch_matrix, sketch_t, root):
    rank, columns = sketch_matrix.shape
    return pl.pallas_call(
        functools.partial(post, root),
        out_shape=(
            jax.ShapeDtypeStruct(sketch_t.shape, jnp.bfloat16),
            jax.ShapeDtypeStruct((rank, columns), jnp.float32),
            jax.ShapeDtypeStruct((rank, rank), jnp.float32),
            jax.ShapeDtypeStruct((rank, rank), jnp.float32),
        ),
        in_specs=[SCALAR] + [VMEM] * 5,
        out_specs=[VMEM] * 4,
        scratch_shapes=[pltpu.VMEM((4 * rank, columns // 2), jnp.bfloat16)],
        compiler_params=pltpu.CompilerParams(vmem_limit_bytes=24 << 20),
        name="factor_and_project",
    )(core, mine_stack, folded, other, sketch_matrix, sketch_t)


def shards(slab, sketch_matrix):
    devices = lax.axis_size("rows")
    core = (lax.axis_index("rows") % 2).reshape(1)
    sketch_t, slab_near, give = begin(core, slab, sketch_matrix)
    shape = give.shape
    got = lax.ppermute(give, "rows", PAIRS)
    keep = keep_half(core, sketch_t, slab_near)
    mine = all_reduce((keep + got).reshape(-1, 8, 128)).reshape(shape)
    other = lax.ppermute(mine, "rows", PAIRS)
    stack, folded = fold_mine(core, mine, sketch_matrix)
    return finish(core, stack, folded, other, sketch_matrix, sketch_t, math.sqrt(slab.shape[0] * devices))


def solution(mesh):
    return jax.shard_map(
        shards,
        mesh=mesh,
        in_specs=(P("rows", None), P()),
        out_specs=(P(None, "rows"), P(), P(), P()),
        check_vma=False,
    )
```

```python
import functools
import math

import jax
import jax.numpy as jnp
from jax import lax
from jax.experimental import pallas as pl
from jax.experimental.pallas import tpu as pltpu
from jax.sharding import PartitionSpec as P

SIZES = dict(z=8, y=8, x=4, c=2)


def place(index):
    coords = {}
    for name in reversed(SIZES):
        index, coords[name] = divmod(index, SIZES[name])
    return coords


def groups(axes_of_core):
    out = {}
    for index in range(math.prod(SIZES.values())):
        coords = place(index)
        axes = axes_of_core[coords["c"]]
        key = (coords["c"],) + tuple(value for name, value in coords.items() if name not in axes)
        out.setdefault(key, []).append(index)
    return list(out.values())


PLANE = groups(("yx", "zx"))
LINE = groups(("z", "y"))
PAIRS = [(i, i ^ 1) for i in range(math.prod(SIZES.values()))]


def exchange(pieces, peers):
    return lax.all_to_all(pieces, "rows", 0, 0, axis_index_groups=peers, tiled=True)


def summed(tiles, count):
    return tiles.reshape(count, tiles.shape[0] // count, 8, 128).sum(0)


def spread(tiles, peers):
    return exchange(jnp.tile(tiles, (len(peers[0]), 1, 1)), peers)


def all_reduce(part):
    part = summed(exchange(part, PLANE), len(PLANE[0]))
    part = summed(spread(part, LINE), len(LINE[0]))
    return spread(part, PLANE)


LAST = (((1,), (1,)), ((), ()))


def split(value, parts):
    out = []
    for _ in range(parts):
        out.append(value.astype(jnp.bfloat16))
        value = value - out[-1].astype(jnp.float32)
    return out


def eliminate(work, base, size=16):
    sub = lax.broadcasted_iota(jnp.int32, (8, 128), 0)

    def row(tile, k):
        return jnp.broadcast_to(tile[k : k + 1, :], (8, 128))

    work = [work[8 * b : 8 * b + 8] for b in range(work.shape[0] // 8)]
    for first in range(0, 8 * len(work), size):
        top, off = divmod(first, 8)
        tops = range(top, (first + size + 7) // 8)
        ends_inside = (first + size) % 8 != 0
        below = range(tops[-1] if ends_inside else tops[-1] + 1, len(work))
        at = base + first
        column = [
            {b: jnp.broadcast_to(work[b][:, at + k : at + k + 1], (8, 128)) for b in range(top, len(work))}
            for k in range(size)
        ]
        pivot = [row(work[(first + k) // 8], (first + k) % 8) for k in range(size)]
        m = {(i, k): row(column[k][(first + i) // 8], (first + i) % 8) for k in range(size) for i in range(k, size)}
        scaled = []
        for k in range(size):
            inverse = 1.0 / m[k, k]
            scaled.append(pivot[k] * inverse)
            x = {i: m[i, k] * inverse for i in range(k + 1, size)}
            for i in x:
                for j in range(k + 1, i + 1):
                    m[i, j] = m[i, j] - x[i] * m[j, k]
                pivot[i] = pivot[i] - x[i] * pivot[k]
                for b in below:
                    column[i][b] = column[i][b] - x[i] * column[k][b]
        new = {}
        for b in below:
            terms = [column[k][b] * scaled[k] for k in range(size)]
            while len(terms) > 1:
                terms = [terms[i] + terms[i + 1] for i in range(0, len(terms), 2)]
            new[b] = work[b] - terms[0]
        for b in tops:
            done = new.get(b, work[b])
            if ends_inside or off:
                done = jnp.where(sub >= off + size, done, work[b])
            for k in range(size):
                if (first + k) // 8 == b:
                    done = jnp.where(sub == (first + k) % 8, pivot[k], done)
            new[b] = done
        for b in new:
            work[b] = new[b]
    return jnp.concatenate(work, 0)


def factor(gram):
    n = gram.shape[0]
    row = lax.broadcasted_iota(jnp.int32, (n, n), 0)
    col = lax.broadcasted_iota(jnp.int32, (n, n), 1)
    on_diag = jnp.where(row == col, gram, 0.0)
    diag_row = jnp.sum(on_diag, 0, keepdims=True)
    down = lax.rsqrt(jnp.sum(on_diag, 1, keepdims=True))
    across = lax.rsqrt(diag_row)
    scale = jnp.where(row == col, jnp.broadcast_to(down, (n, n)), 0.0)
    work = jnp.concatenate([gram * down * across, scale], 1)
    work = eliminate(work, 0)
    upper = work[:, :n]
    left = lax.rsqrt(jnp.sum(jnp.where(row == col, upper, 0.0), 1, keepdims=True))
    return jnp.where(col >= row, upper * left * (diag_row * across), 0.0), work[:, n:] * left


def pre(widths, core_ref, slab_hbm, sketch_hbm, sketch_t_ref, slab_ref, give_ref, sketch_ref, arrived):
    views, at = [], 0
    for width in widths:
        views.append(pl.ds(at, width))
        at += width
    copies = [
        [
            pltpu.make_async_copy(source.at[:, view], target.at[:, view], arrived.at[j, i])
            for j, (source, target) in enumerate(((sketch_hbm, sketch_ref), (slab_hbm, slab_ref)))
        ]
        for i, view in enumerate(views)
    ]
    for pair in copies:
        for copy in pair:
            copy.start()
    sketch_t = jnp.zeros(sketch_t_ref.shape, jnp.float32)
    for pair, view in zip(copies, views):
        for copy in pair:
            copy.wait()
        sketch_t += lax.dot_general(
            sketch_ref[:, view], slab_ref[:, view], LAST, preferred_element_type=jnp.float32
        )
    sketch_t_ref[...] = sketch_t
    cross_half(1 - core_ref[0], sketch_t, slab_ref, give_ref)


def cross_half(which, sketch_t, slab_ref, out_ref):
    half = slab_ref.shape[1] // 2
    view = pl.ds(pl.multiple_of(which * half, half), half)
    part = jnp.dot(sketch_t.astype(jnp.bfloat16), slab_ref[:, view], preferred_element_type=jnp.float32)
    for b in range(half // 128):
        out_ref[b] = part[:, b * 128 : (b + 1) * 128]


def pre_keep(core_ref, sketch_t_ref, slab_ref, keep_ref):
    cross_half(core_ref[0], sketch_t_ref[...], slab_ref, keep_ref)


SCALAR = pl.BlockSpec(memory_space=pltpu.SMEM)
VMEM = pl.BlockSpec(memory_space=pltpu.VMEM)
LIMIT = pltpu.CompilerParams(vmem_limit_bytes=16 << 20)


def begin(core, slab, sketch_matrix):
    rows, columns = slab.shape
    widths = [columns * part // 16 for part in (1, 3, 5, 7)]
    rank = sketch_matrix.shape[0]
    slab, sketch_matrix = (pltpu.with_memory_space_constraint(a, pltpu.HBM) for a in (slab, sketch_matrix))
    hbm = pl.BlockSpec(memory_space=pltpu.HBM)
    return pl.pallas_call(
        functools.partial(pre, widths),
        out_shape=(
            pltpu.VMEM((rank, rows), jnp.float32),
            pltpu.VMEM(slab.shape, slab.dtype),
            pltpu.VMEM((columns // 256, rank, 128), jnp.float32),
        ),
        in_specs=[SCALAR, hbm, hbm],
        out_specs=[VMEM] * 3,
        scratch_shapes=[
            pltpu.VMEM(sketch_matrix.shape, sketch_matrix.dtype),
            pltpu.SemaphoreType.DMA((2, len(widths))),
        ],
        compiler_params=LIMIT,
        name="sketch_and_cross_to_give",
    )(core, slab, sketch_matrix)


def keep_half(core, sketch_t, slab):
    rows, columns = slab.shape
    rank = sketch_t.shape[0]
    return pl.pallas_call(
        pre_keep,
        out_shape=pltpu.VMEM((columns // 256, rank, 128), jnp.float32),
        in_specs=[SCALAR, VMEM, VMEM],
        out_specs=VMEM,
        compiler_params=LIMIT,
        cost_estimate=pl.CostEstimate(flops=rank * rows * columns, bytes_accessed=slab.size, transcendentals=0),
        name="cross_to_keep",
    )(core, sketch_t, slab)


def right_parts(value):
    high, mid, low = split(value, 3)
    return jnp.concatenate([high, mid, low, high], 0)


def left_parts(value):
    high, mid, low = split(value, 3)
    zero = jnp.zeros_like(high)
    rows = ((high, high, high, low), (mid, mid, zero, zero))
    return jnp.concatenate([jnp.concatenate(parts, 1) for parts in rows], 0)


def fold_half(which, source, sketch_ref, stack):
    rank = sketch_ref.shape[0]
    half = source.shape[0] * 128
    cross = jnp.concatenate([source[b] for b in range(source.shape[0])], 1)
    stack[...] = right_parts(cross)
    view = pl.ds(pl.multiple_of(which * half, half), half)
    out = lax.dot_general(stack[: 3 * rank], sketch_ref[:, view], LAST, preferred_element_type=jnp.float32)
    return out[:rank] + (out[rank : 2 * rank] + out[2 * rank :])


def post_mine(core_ref, mine_ref, sketch_ref, stack, folded_ref):
    folded_ref[...] = fold_half(core_ref[0], mine_ref, sketch_ref, stack)


def fold_mine(core, mine, sketch_matrix):
    rank, columns = sketch_matrix.shape
    return pl.pallas_call(
        post_mine,
        out_shape=(
            pltpu.VMEM((4 * rank, columns // 2), jnp.bfloat16),
            pltpu.VMEM((rank, rank), jnp.float32),
        ),
        in_specs=[SCALAR, VMEM, VMEM],
        out_specs=[VMEM] * 2,
        compiler_params=LIMIT,
        cost_estimate=pl.CostEstimate(
            flops=3 * rank * rank * columns, bytes_accessed=4 * rank * columns, transcendentals=0
        ),
        name="fold_mine",
    )(core, mine, sketch_matrix)


def post(
    root, core_ref, mine_stack, folded_ref, other_ref, sketch_ref, sketch_t_ref, q_ref, proj_ref, tri_ref, gram_ref, other_stack
):
    rank, columns = proj_ref.shape
    half = columns // 2
    core = core_ref[0]
    folded = folded_ref[...] + fold_half(1 - core, other_ref, sketch_ref, other_stack)
    upper, inverse = factor(0.5 * (folded + folded.T))
    tri_ref[...] = upper * (1.0 / root)
    left = left_parts(inverse)
    total = jnp.zeros((2 * rank, rank), jnp.float32)
    for which, stack in ((core, mine_stack), (1 - core, other_stack)):
        for at in range(0, half, 512):
            part = jnp.dot(left, stack[:, at : at + 512], preferred_element_type=jnp.float32)
            part = part[:rank] + part[rank:]
            proj_ref[:, pl.ds(pl.multiple_of(which * half + at, 128), 512)] = part
            pair = split(part, 2)
            total += lax.dot_general(
                jnp.concatenate(pair, 0), pair[0], LAST, preferred_element_type=jnp.float32
            )
    gram_ref[...] = (total[:rank] + (total[rank:] + total[rank:].T)) * (1.0 / columns)
    part = jnp.dot(left_parts(inverse * root), right_parts(sketch_t_ref[...]), preferred_element_type=jnp.float32)
    q_ref[...] = (part[:rank] + part[rank:]).astype(q_ref.dtype)


def finish(core, mine_stack, folded, other, sketch_matrix, sketch_t, root):
    rank, columns = sketch_matrix.shape
    return pl.pallas_call(
        functools.partial(post, root),
        out_shape=(
            jax.ShapeDtypeStruct(sketch_t.shape, jnp.bfloat16),
            jax.ShapeDtypeStruct((rank, columns), jnp.float32),
            jax.ShapeDtypeStruct((rank, rank), jnp.float32),
            jax.ShapeDtypeStruct((rank, rank), jnp.float32),
        ),
        in_specs=[SCALAR] + [VMEM] * 5,
        out_specs=[VMEM] * 4,
        scratch_shapes=[pltpu.VMEM((4 * rank, columns // 2), jnp.bfloat16)],
        compiler_params=pltpu.CompilerParams(vmem_limit_bytes=24 << 20),
        name="factor_and_project",
    )(core, mine_stack, folded, other, sketch_matrix, sketch_t)


def shards(slab, sketch_matrix):
    devices = lax.axis_size("rows")
    core = (lax.axis_index("rows") % 2).reshape(1)
    sketch_t, slab_near, give = begin(core, slab, sketch_matrix)
    shape = give.shape
    got = lax.ppermute(give, "rows", PAIRS)
    keep = keep_half(core, sketch_t, slab_near)
    mine = all_reduce((keep + got).reshape(-1, 8, 128)).reshape(shape)
    other = lax.ppermute(mine, "rows", PAIRS)
    stack, folded = fold_mine(core, mine, sketch_matrix)
    return finish(core, stack, folded, other, sketch_matrix, sketch_t, math.sqrt(slab.shape[0] * devices))


def solution(mesh):
    return jax.shard_map(
        shards,
        mesh=mesh,
        in_specs=(P("rows", None), P()),
        out_specs=(P(None, "rows"), P(), P(), P()),
        check_vma=False,
    )
```

```python
import functools
import math

import jax
import jax.numpy as jnp
from jax import lax
from jax.experimental import pallas as pl
from jax.experimental.pallas import tpu as pltpu
from jax.sharding import PartitionSpec as P

SIZES = dict(z=8, y=8, x=4, c=2)


def place(index):
    coords = {}
    for name in reversed(SIZES):
        index, coords[name] = divmod(index, SIZES[name])
    return coords


def groups(axes_of_core):
    out = {}
    for index in range(math.prod(SIZES.values())):
        coords = place(index)
        axes = axes_of_core[coords["c"]]
        key = (coords["c"],) + tuple(value for name, value in coords.items() if name not in axes)
        out.setdefault(key, []).append(index)
    return list(out.values())


PLANE = groups(("yx", "zx"))
LINE = groups(("z", "y"))
PAIRS = [(i, i ^ 1) for i in range(math.prod(SIZES.values()))]


def exchange(pieces, peers):
    return lax.all_to_all(pieces, "rows", 0, 0, axis_index_groups=peers, tiled=True)


def summed(tiles, count):
    return tiles.reshape(count, tiles.shape[0] // count, 8, 128).sum(0)


def spread(tiles, peers):
    return exchange(jnp.tile(tiles, (len(peers[0]), 1, 1)), peers)


def all_reduce(part):
    part = summed(exchange(part, PLANE), len(PLANE[0]))
    part = summed(spread(part, LINE), len(LINE[0]))
    return spread(part, PLANE)


LAST = (((1,), (1,)), ((), ()))


def split(value, parts):
    out = []
    for _ in range(parts):
        out.append(value.astype(jnp.bfloat16))
        value = value - out[-1].astype(jnp.float32)
    return out


def eliminate(work, base, size=16):
    sub = lax.broadcasted_iota(jnp.int32, (8, 128), 0)

    def row(tile, k):
        return jnp.broadcast_to(tile[k : k + 1, :], (8, 128))

    work = [work[8 * b : 8 * b + 8] for b in range(work.shape[0] // 8)]
    for first in range(0, 8 * len(work), size):
        top, off = divmod(first, 8)
        tops = range(top, (first + size + 7) // 8)
        ends_inside = (first + size) % 8 != 0
        below = range(tops[-1] if ends_inside else tops[-1] + 1, len(work))
        at = base + first
        column = [
            {b: jnp.broadcast_to(work[b][:, at + k : at + k + 1], (8, 128)) for b in range(top, len(work))}
            for k in range(size)
        ]
        pivot = [row(work[(first + k) // 8], (first + k) % 8) for k in range(size)]
        m = {(i, k): row(column[k][(first + i) // 8], (first + i) % 8) for k in range(size) for i in range(k, size)}
        scaled = []
        for k in range(size):
            inverse = 1.0 / m[k, k]
            scaled.append(pivot[k] * inverse)
            x = {i: m[i, k] * inverse for i in range(k + 1, size)}
            for i in x:
                for j in range(k + 1, i + 1):
                    m[i, j] = m[i, j] - x[i] * m[j, k]
                pivot[i] = pivot[i] - x[i] * pivot[k]
                for b in below:
                    column[i][b] = column[i][b] - x[i] * column[k][b]
        new = {}
        for b in below:
            terms = [column[k][b] * scaled[k] for k in range(size)]
            while len(terms) > 1:
                terms = [terms[i] + terms[i + 1] for i in range(0, len(terms), 2)]
            new[b] = work[b] - terms[0]
        for b in tops:
            done = new.get(b, work[b])
            if ends_inside or off:
                done = jnp.where(sub >= off + size, done, work[b])
            for k in range(size):
                if (first + k) // 8 == b:
                    done = jnp.where(sub == (first + k) % 8, pivot[k], done)
            new[b] = done
        for b in new:
            work[b] = new[b]
    return jnp.concatenate(work, 0)


def factor(gram):
    n = gram.shape[0]
    row = lax.broadcasted_iota(jnp.int32, (n, n), 0)
    col = lax.broadcasted_iota(jnp.int32, (n, n), 1)
    on_diag = jnp.where(row == col, gram, 0.0)
    diag_row = jnp.sum(on_diag, 0, keepdims=True)
    down = lax.rsqrt(jnp.sum(on_diag, 1, keepdims=True))
    across = lax.rsqrt(diag_row)
    scale = jnp.where(row == col, jnp.broadcast_to(down, (n, n)), 0.0)
    work = jnp.concatenate([gram * down * across, scale], 1)
    work = eliminate(work, 0)
    upper = work[:, :n]
    left = lax.rsqrt(jnp.sum(jnp.where(row == col, upper, 0.0), 1, keepdims=True))
    return jnp.where(col >= row, upper * left * (diag_row * across), 0.0), work[:, n:] * left


def pre(widths, core_ref, slab_hbm, sketch_hbm, sketch_t_ref, slab_ref, give_ref, sketch_ref, arrived):
    views, at = [], 0
    for width in widths:
        views.append(pl.ds(at, width))
        at += width
    copies = [
        [
            pltpu.make_async_copy(source.at[:, view], target.at[:, view], arrived.at[j, i])
            for j, (source, target) in enumerate(((sketch_hbm, sketch_ref), (slab_hbm, slab_ref)))
        ]
        for i, view in enumerate(views)
    ]
    for pair in copies:
        for copy in pair:
            copy.start()
    sketch_t = jnp.zeros(sketch_t_ref.shape, jnp.float32)
    for pair, view in zip(copies, views):
        for copy in pair:
            copy.wait()
        sketch_t += lax.dot_general(
            sketch_ref[:, view], slab_ref[:, view], LAST, preferred_element_type=jnp.float32
        )
    sketch_t_ref[...] = sketch_t
    cross_half(1 - core_ref[0], sketch_t, slab_ref, give_ref)


def cross_half(which, sketch_t, slab_ref, out_ref):
    half = slab_ref.shape[1] // 2
    view = pl.ds(pl.multiple_of(which * half, half), half)
    part = jnp.dot(sketch_t.astype(jnp.bfloat16), slab_ref[:, view], preferred_element_type=jnp.float32)
    for b in range(half // 128):
        out_ref[b] = part[:, b * 128 : (b + 1) * 128]


def pre_keep(core_ref, sketch_t_ref, slab_ref, keep_ref):
    cross_half(core_ref[0], sketch_t_ref[...], slab_ref, keep_ref)


SCALAR = pl.BlockSpec(memory_space=pltpu.SMEM)
VMEM = pl.BlockSpec(memory_space=pltpu.VMEM)
LIMIT = pltpu.CompilerParams(vmem_limit_bytes=16 << 20)


def begin(core, slab, sketch_matrix):
    rows, columns = slab.shape
    widths = [columns * part // 16 for part in (1, 3, 5, 7)]
    rank = sketch_matrix.shape[0]
    slab, sketch_matrix = (pltpu.with_memory_space_constraint(a, pltpu.HBM) for a in (slab, sketch_matrix))
    hbm = pl.BlockSpec(memory_space=pltpu.HBM)
    return pl.pallas_call(
        functools.partial(pre, widths),
        out_shape=(
            pltpu.VMEM((rank, rows), jnp.float32),
            pltpu.VMEM(slab.shape, slab.dtype),
            pltpu.VMEM((columns // 256, rank, 128), jnp.float32),
        ),
        in_specs=[SCALAR, hbm, hbm],
        out_specs=[VMEM] * 3,
        scratch_shapes=[
            pltpu.VMEM(sketch_matrix.shape, sketch_matrix.dtype),
            pltpu.SemaphoreType.DMA((2, len(widths))),
        ],
        compiler_params=LIMIT,
        name="sketch_and_cross_to_give",
    )(core, slab, sketch_matrix)


def keep_half(core, sketch_t, slab):
    rows, columns = slab.shape
    rank = sketch_t.shape[0]
    return pl.pallas_call(
        pre_keep,
        out_shape=pltpu.VMEM((columns // 256, rank, 128), jnp.float32),
        in_specs=[SCALAR, VMEM, VMEM],
        out_specs=VMEM,
        compiler_params=LIMIT,
        cost_estimate=pl.CostEstimate(flops=rank * rows * columns, bytes_accessed=slab.size, transcendentals=0),
        name="cross_to_keep",
    )(core, sketch_t, slab)


def right_parts(value):
    high, mid, low = split(value, 3)
    return jnp.concatenate([high, mid, low, high], 0)


def left_parts(value):
    high, mid, low = split(value, 3)
    zero = jnp.zeros_like(high)
    rows = ((high, high, high, low), (mid, mid, zero, zero))
    return jnp.concatenate([jnp.concatenate(parts, 1) for parts in rows], 0)


def fold_half(which, source, sketch_ref, stack):
    rank = sketch_ref.shape[0]
    half = source.shape[0] * 128
    cross = jnp.concatenate([source[b] for b in range(source.shape[0])], 1)
    stack[...] = right_parts(cross)
    view = pl.ds(pl.multiple_of(which * half, half), half)
    out = lax.dot_general(stack[: 3 * rank], sketch_ref[:, view], LAST, preferred_element_type=jnp.float32)
    return out[:rank] + (out[rank : 2 * rank] + out[2 * rank :])


def post_mine(core_ref, mine_ref, sketch_ref, stack, folded_ref):
    folded_ref[...] = fold_half(core_ref[0], mine_ref, sketch_ref, stack)


def fold_mine(core, mine, sketch_matrix):
    rank, columns = sketch_matrix.shape
    return pl.pallas_call(
        post_mine,
        out_shape=(
            pltpu.VMEM((4 * rank, columns // 2), jnp.bfloat16),
            pltpu.VMEM((rank, rank), jnp.float32),
        ),
        in_specs=[SCALAR, VMEM, VMEM],
        out_specs=[VMEM] * 2,
        compiler_params=LIMIT,
        cost_estimate=pl.CostEstimate(
            flops=3 * rank * rank * columns, bytes_accessed=4 * rank * columns, transcendentals=0
        ),
        name="fold_mine",
    )(core, mine, sketch_matrix)


def post(
    root, core_ref, mine_stack, folded_ref, other_ref, sketch_ref, sketch_t_ref, q_ref, proj_ref, tri_ref, gram_ref, other_stack
):
    rank, columns = proj_ref.shape
    half = columns // 2
    core = core_ref[0]
    folded = folded_ref[...] + fold_half(1 - core, other_ref, sketch_ref, other_stack)
    upper, inverse = factor(0.5 * (folded + folded.T))
    tri_ref[...] = upper * (1.0 / root)
    part = jnp.dot(left_parts(inverse * root), right_parts(sketch_t_ref[...]), preferred_element_type=jnp.float32)
    q_ref[...] = (part[:rank] + part[rank:]).astype(q_ref.dtype)
    left = left_parts(inverse)
    total = jnp.zeros((2 * rank, rank), jnp.float32)
    for which, stack in ((core, mine_stack), (1 - core, other_stack)):
        for at in range(0, half, 512):
            part = jnp.dot(left, stack[:, at : at + 512], preferred_element_type=jnp.float32)
            part = part[:rank] + part[rank:]
            proj_ref[:, pl.ds(pl.multiple_of(which * half + at, 128), 512)] = part
            pair = split(part, 2)
            total += lax.dot_general(
                jnp.concatenate(pair, 0), pair[0], LAST, preferred_element_type=jnp.float32
            )
    gram_ref[...] = (total[:rank] + (total[rank:] + total[rank:].T)) * (1.0 / columns)


def finish(core, mine_stack, folded, other, sketch_matrix, sketch_t, root):
    rank, columns = sketch_matrix.shape
    return pl.pallas_call(
        functools.partial(post, root),
        out_shape=(
            jax.ShapeDtypeStruct(sketch_t.shape, jnp.bfloat16),
            jax.ShapeDtypeStruct((rank, columns), jnp.float32),
            jax.ShapeDtypeStruct((rank, rank), jnp.float32),
            jax.ShapeDtypeStruct((rank, rank), jnp.float32),
        ),
        in_specs=[SCALAR] + [VMEM] * 5,
        out_specs=[VMEM] * 4,
        scratch_shapes=[pltpu.VMEM((4 * rank, columns // 2), jnp.bfloat16)],
        compiler_params=pltpu.CompilerParams(vmem_limit_bytes=24 << 20),
        name="factor_and_project",
    )(core, mine_stack, folded, other, sketch_matrix, sketch_t)


def shards(slab, sketch_matrix):
    devices = lax.axis_size("rows")
    core = (lax.axis_index("rows") % 2).reshape(1)
    sketch_t, slab_near, give = begin(core, slab, sketch_matrix)
    shape = give.shape
    got = lax.ppermute(give, "rows", PAIRS)
    keep = keep_half(core, sketch_t, slab_near)
    mine = all_reduce((keep + got).reshape(-1, 8, 128)).reshape(shape)
    other = lax.ppermute(mine, "rows", PAIRS)
    stack, folded = fold_mine(core, mine, sketch_matrix)
    return finish(core, stack, folded, other, sketch_matrix, sketch_t, math.sqrt(slab.shape[0] * devices))


def solution(mesh):
    return jax.shard_map(
        shards,
        mesh=mesh,
        in_specs=(P("rows", None), P()),
        out_specs=(P(None, "rows"), P(), P(), P()),
        check_vma=False,
    )
```
